256 devices in a mesh: row: 16 (over z, core), col: 4 (over x), layer: 4 (over y).
Axes of the slice: x: 4, y: 4, z: 8, core: 2. Of those that a mesh axis runs over, the one named last changes fastest.
Arguments:
- ks_owned: float32 [1024, 16, 64, 64], P(('row', 'col'), 'layer'), may hold values from -0.4375 to 0.4375
- owned_rows: int32 [1024], P(('row', 'col')), may hold values from -1 to 383, as said below
- left_cols: int32 [384, 16], P('row', 'layer'), may hold values from 0 to 383, as said below
- right_blocks: float32 [384, 16, 64, 64], P(('layer', 'row'), 'col'), may hold values from -6 to 6
- right_cols: int32 [384, 16], P('layer', 'col'), may hold values from 0 to 383, as said below
- kept_cols: int32 [384, 32], P('row', 'col'), may hold values from 0 to 383, as said below
Outputs:
- product_blocks: float32 [384, 32, 64, 64], P(('row', 'layer'), 'col')
The draws below stay inside these ranges and needn't reach their ends.
Inputs may be any that keep to these rules, and one draw needn't show every extreme that they name: `owned_rows`: slot s belongs to owner s // 16, at grid row (s // 16) // 4 and grid column (s // 16) % 4. Block row i belongs to cell i // 6, at grid row (i // 6) // 4 and grid column (i // 6) % 4. Every block row is held in exactly one slot, by an owner in its cell's grid column; all other slots hold -1. An owner holds at most 1 block rows of one cell, and in every draw some owner of every grid column holds 1 block rows of each cell of that column, 16 in all. `left_cols`: slots l * 4 to (l + 1) * 4 - 1 of each block row hold distinct block columns from l * 96 to (l + 1) * 96 - 1. `right_cols`: slots c * 4 to (c + 1) * 4 - 1 of each block row hold distinct block columns from c * 96 to (c + 1) * 96 - 1. `kept_cols`: slots c * 8 to (c + 1) * 8 - 1 of each block row hold distinct block columns from c * 96 to (c + 1) * 96 - 1.
All inputs are finite; a program needn't handle non-finite values.
Results may differ from the reference program's by a relative error of at most 0.0003.
Values sent between devices are 32-bit elements; how exact they have to be, the bound alone decides.
No kernel may reach another device: no remote copies, remote signals or barrier semaphores. Data moves between devices by JAX's collectives and lax.ppermute only.
A program may use at most 128 MiB of HBM per device.

```python
import jax
import jax.numpy as jnp
from jax import lax

BS = 64
CELL_ROWS = 6
KAL = 4
KBC = 4
KCC = 8
GRID_ROWS = 16
GRID_COLS = 4
LAYERS = 4
NB = 384
INNER = 96
COLS = 96
KA = 16
KB = 16
SEND_CAP = 1
OWN_CAP = 16
HEAVY = 4


def column_sets(base_key, row_total, groups, spread, picks):
    key_list = jax.random.split(base_key, row_total * groups)
    chosen = jax.vmap(lambda single: jax.random.permutation(single, spread)[:picks])(key_list)
    chosen = chosen.reshape(row_total, groups, picks) + (jnp.arange(groups) * spread)[None, :, None]
    return chosen.reshape(row_total, groups * picks).astype(jnp.int32)


def draw_left_cols(key, part):
    return column_sets(jax.random.fold_in(key, 11), NB, LAYERS, INNER, KAL)


def draw_right_cols(key, part):
    return column_sets(jax.random.fold_in(key, 12), NB, GRID_COLS, COLS, KBC)


def draw_kept_cols(key, part):
    return column_sets(jax.random.fold_in(key, 13), NB, GRID_COLS, COLS, KCC)


def draw_owned_rows(key, part):
    first_key, second_key, third_key = jax.random.split(jax.random.fold_in(key, 21), 3)
    cell_total = GRID_ROWS * GRID_COLS
    row_index = jnp.arange(NB)
    cell_index = row_index // CELL_ROWS
    shuffle = jax.vmap(lambda single: jax.random.permutation(single, CELL_ROWS))(jax.random.split(first_key, cell_total))
    within = shuffle[cell_index, row_index % CELL_ROWS]
    grid_row = cell_index // GRID_COLS
    grid_col = cell_index % GRID_COLS
    heavy_rows = HEAVY * SEND_CAP
    is_heavy = within < heavy_rows
    light_rank = within - heavy_rows
    light_owner = HEAVY + (light_rank // SEND_CAP + grid_row) % (GRID_ROWS - HEAVY)
    local_owner = jnp.where(is_heavy, within // SEND_CAP, light_owner)
    position = grid_row * SEND_CAP + jnp.where(is_heavy, within % SEND_CAP, light_rank % SEND_CAP)
    owner_order = jax.vmap(lambda single: jax.random.permutation(single, GRID_ROWS))(jax.random.split(second_key, GRID_COLS))
    owner_index = owner_order[grid_col, local_owner] * GRID_COLS + grid_col
    slot_order = jax.vmap(lambda single: jax.random.permutation(single, OWN_CAP))(jax.random.split(third_key, cell_total))
    slot_index = owner_index * OWN_CAP + slot_order[owner_index, position]
    empty_slots = jnp.full((cell_total * OWN_CAP,), -1, jnp.int32)
    return empty_slots.at[slot_index].set(row_index.astype(jnp.int32))


def steps_of(key, extent, cuts, least, largest):
    def one(dim, parts):
        heights = jax.random.uniform(jax.random.fold_in(jax.random.fold_in(key, 6), dim), (parts,), jnp.float32, least / len(cuts), largest / len(cuts))
        return jnp.repeat(jnp.exp(heights), extent[dim] // parts).reshape((-1,) + (1,) * (len(extent) - dim - 1))

    factor_of = one(*cuts[0])
    for cut in cuts[1:]:
        factor_of = factor_of * one(*cut)
    return factor_of


def centred(stream_key, dims, scale, most, cuts=(), kind=jnp.bfloat16):
    array = jax.random.normal(stream_key, dims, jnp.float32) * scale
    if len(cuts) > 0:
        array = steps_of(stream_key, dims, cuts, -0.22, 0.18) * array
    return jnp.clip(array, min=-most, max=most).astype(kind)


def setup_inputs(seed: int = 0) -> dict:
    seeds = jax.random.split(jax.random.key(seed), 7)
    return {
        "ks_owned": centred(seeds[0], (GRID_ROWS * GRID_COLS * OWN_CAP, KA, BS, BS), (3 * BS) ** -0.5, 0.4375, ((0, 64), (1, 4)), jnp.float32),
        "owned_rows": draw_owned_rows(jax.random.fold_in(seeds[6], 71), 0),
        "left_cols": draw_left_cols(jax.random.fold_in(seeds[6], 71), 0),
        "right_blocks": centred(seeds[3], (NB, KB, BS, BS), 1.0, 6.0, ((0, 64), (1, 4)), jnp.float32),
        "right_cols": draw_right_cols(jax.random.fold_in(seeds[6], 71), 0),
        "kept_cols": draw_kept_cols(jax.random.fold_in(seeds[6], 71), 0),
    }


def reference(ks_owned, owned_rows, left_cols, right_blocks, right_cols, kept_cols):
    target = jnp.where(owned_rows >= 0, owned_rows, NB)
    left_blocks = jnp.zeros((NB,) + ks_owned.shape[1:], ks_owned.dtype).at[target].set(ks_owned, mode="drop")

    def row_product(packed_row):
        left_row, inner_ids, wanted = packed_row
        picked = right_blocks[inner_ids]
        picked_cols = right_cols[inner_ids]
        products = jnp.einsum("kab,klbc->klac", left_row, picked, precision=lax.Precision.HIGHEST)
        matches = (picked_cols[:, :, None] == wanted[None, None, :]).astype(left_row.dtype)
        return jnp.einsum("klq,klac->qac", matches, products, precision=lax.Precision.HIGHEST)

    return lax.map(row_product, (left_blocks, left_cols, kept_cols))
```

```python
import functools

import jax
import jax.numpy as jnp
from jax import lax
from jax.experimental import pallas as pl
from jax.experimental.pallas import tpu as pltpu
from jax.sharding import PartitionSpec as P

VMEM = pltpu.VMEM
SMEM = pltpu.SMEM
GROUP = 4
DEPTH = 16
CHUNKS = (2, 1, 3, 0)
F32 = jnp.float32
BF16 = jnp.bfloat16


def vspec():
    return pl.BlockSpec(memory_space=VMEM)


def sspec():
    return pl.BlockSpec(memory_space=SMEM)


def aspec():
    return pl.BlockSpec(memory_space=pl.ANY)


def folded(block):
    half = block.shape[0] // 2
    return jnp.concatenate([block[:half], block[half:]], axis=1)


def pack_right_kernel(blocks_ref, out_ref):
    rows, slots = blocks_ref.shape[:2]
    for i in range(rows):
        for k in range(slots):
            out_ref[i * slots + k] = folded(blocks_ref[i, k])


def pack_left_kernel(span, owned_ref, blocks_ref, out_ref, slot_of):
    slots, parts, size = blocks_ref.shape[:3]
    groups = out_ref.shape[0]
    half = size // 2

    def clear(g, carry):
        slot_of[g] = -1
        return carry

    def find(s, carry):
        row = owned_ref[s]

        @pl.when(row >= 0)
        def _():
            slot_of[row // span] = s

        return carry

    def fill(g, carry):
        slot = slot_of[g]
        at = jnp.maximum(slot, 0)
        number = jnp.where(slot >= 0, owned_ref[at], -1).astype(F32)
        out_ref[g, parts * half :, :] = jnp.full((out_ref.shape[1] - parts * half, 2 * size), number, F32)
        for k in range(parts):
            out_ref[g, k * half : (k + 1) * half, :] = folded(blocks_ref[at, k])
        return carry

    lax.fori_loop(0, groups, clear, 0)
    lax.fori_loop(0, slots, find, 0)
    lax.fori_loop(0, groups, fill, 0)


def compact_kernel(span, arrived_ref, out_ref):
    sources = arrived_ref.shape[0]
    body = out_ref.shape[1]
    cell = out_ref.shape[0]
    first = lax.axis_index("row") * span + lax.axis_index("col") * cell
    numbers = [jnp.max(arrived_ref[s, body:, :]).astype(jnp.int32) for s in range(sources)]
    for s in range(sources):
        place = numbers[s] - first

        @pl.when(numbers[s] >= 0)
        def _(s=s, place=place):
            out_ref[place] = arrived_ref[s, :body, :]


def pairs_kernel(left_ref, right_ref, kept_ref, list_ref, start_ref, table):
    parts, rows = left_ref.shape
    terms, inner = right_ref.shape
    kept = kept_ref.shape[0]
    layers = len(CHUNKS)
    cell = rows // layers
    layer = lax.axis_index("layer")
    left_first = layer * inner
    right_first = lax.axis_index("col") * table.shape[0]

    def clear(i, carry):
        table[i] = -1
        return carry

    lax.fori_loop(0, table.shape[0], clear, 0)
    count = 0
    for t, distance in enumerate(CHUNKS):
        start_ref[t] = count
        base = lax.rem(layer + distance, layers) * cell

        def one_row(p, count, base=base):
            r = base + p
            for q in range(kept):
                table[kept_ref[q, r] - right_first] = q
            for k in range(parts):
                j = left_ref[k, r] - left_first
                for l in range(terms):
                    q = table[right_ref[l, j] - right_first]
                    code = (r * parts + k) + (j * terms + l) * 128 + (p * kept + q) * 65536
                    list_ref[count] = code
                    count = count + (q >= 0).astype(jnp.int32)
            for q in range(kept):
                table[kept_ref[q, r] - right_first] = -1
            return count

        count = lax.fori_loop(0, cell, one_row, count)
    start_ref[layers] = count
    for i in range(DEPTH + GROUP):
        list_ref[count + i] = 0


def product_kernel(chunks, list_ref, start_ref, *refs):
    left_refs = refs[:4]
    right_ref = refs[4]
    n_out = len(refs) - 9
    out_refs = refs[5 : 5 + n_out]
    left, ring, left_sems, ring_sems = refs[5 + n_out :]
    first, last = chunks[0][0], chunks[-1][0]
    per_source = left_refs[0].shape[0]
    col = lax.axis_index("col")
    copies = []
    for o in range(4):
        at = lax.rem(col + o, 4) * per_source
        copies.append(pltpu.make_async_copy(left_refs[o], left.at[pl.ds(at, per_source)], left_sems.at[o]))
        copies[-1].start()
    begin = start_ref[first]
    end = start_ref[last + 1]

    def fetch(i):
        code = list_ref[i]
        block = lax.rem(lax.shift_right_logical(code, 7), 512)
        slot = lax.rem(i, DEPTH)
        return pltpu.make_async_copy(right_ref.at[block], ring.at[slot], ring_sems.at[slot])

    def prime(i, carry):
        fetch(i).start()
        return carry

    lax.fori_loop(begin, jnp.minimum(begin + DEPTH, end), prime, 0)
    for _, targets in chunks:
        for ref, _ in targets:
            ref[...] = jnp.zeros_like(ref)
    for copy in copies:
        copy.wait()
    lane = lax.broadcasted_iota(jnp.int32, (32, 128), 1)
    low = lane < 64

    def product(i):
        code = list_ref[i]
        a = left[lax.rem(code, 128)]
        b = ring[lax.rem(i, DEPTH)]
        turned = pltpu.roll(b, 64, 1)
        wide = jnp.concatenate(
            [
                jnp.where(low, b, 0.0),
                jnp.where(low, turned, 0.0),
                jnp.where(low, 0.0, turned),
                jnp.where(low, 0.0, b),
            ],
            axis=0,
        )
        a_hi = a.astype(BF16)
        a_lo = (a - a_hi.astype(F32)).astype(BF16)
        w_hi = wide.astype(BF16)
        w_lo = (wide - w_hi.astype(F32)).astype(BF16)
        main = jnp.dot(a_hi, w_hi, preferred_element_type=F32)
        rest = jnp.dot(a_lo, w_hi, preferred_element_type=F32) + jnp.dot(
            a_hi, w_lo, preferred_element_type=F32
        )
        return main + rest

    for t, targets in chunks:
        stop = start_ref[t + 1]
        start = start_ref[t]

        def group(g, carry, stop=stop, start=start, targets=targets):
            base = start + g * GROUP
            for u in range(GROUP):

                @pl.when(base + u < stop)
                def _(u=u):
                    fetch(base + u).wait()

            values = [product(jnp.minimum(base + u, stop - 1)) for u in range(GROUP)]
            for u in range(GROUP):

                @pl.when((base + u < stop) & (base + u + DEPTH < end))
                def _(u=u):
                    fetch(base + u + DEPTH).start()

            for u in range(GROUP):
                spot = lax.shift_right_logical(list_ref[base + u], 16)
                for ref, (lo, hi) in targets:

                    @pl.when((base + u < stop) & (spot >= lo) & (spot < hi))
                    def _(u=u, ref=ref, lo=lo, spot=spot):
                        ref[spot - lo] += values[u]

            return carry

        lax.fori_loop(0, lax.div(stop - start + GROUP - 1, GROUP), group, 0)


def final_kernel(own_ref, a0, a1, b0, b1, out_ref):
    rows, kept, size = out_ref.shape[:3]
    half = size // 2
    per = a0.shape[0]

    for i in range(rows * kept):
        p, q = i // kept, i % kept
        x, y = (a0, b0) if i < per else (a1, b1)
        total = own_ref[i] + x[i % per] + y[i % per]
        out_ref[p, q, :half, :] = total[:, :size]
        out_ref[p, q, half:, :] = total[:, size:]


def shards(ks_owned, owned_rows, left_cols, right_blocks, right_cols, kept_cols):
    rows_axis = lax.axis_size("row")
    cols_axis = lax.axis_size("col")
    layers = lax.axis_size("layer")
    slots, parts, size = ks_owned.shape[:3]
    half, wide = size // 2, size * 2
    panel = left_cols.shape[0]
    cell = panel // cols_axis
    inner, terms = right_cols.shape
    kept = kept_cols.shape[1]
    body = parts * half
    sds = jax.ShapeDtypeStruct

    right = pl.pallas_call(
        pack_right_kernel,
        out_shape=sds((right_blocks.shape[0] * terms, half, wide), F32),
        in_specs=[vspec()],
        out_specs=vspec(),
        name="pack_right",
    )(right_blocks)
    right_all = lax.all_gather(right, "row", axis=0, tiled=True)

    packed = pl.pallas_call(
        functools.partial(pack_left_kernel, panel),
        out_shape=sds((rows_axis, body + 8, wide), F32),
        in_specs=[sspec(), vspec()],
        out_specs=vspec(),
        scratch_shapes=[SMEM((rows_axis,), jnp.int32)],
        name="pack_left",
    )(owned_rows, ks_owned)
    arrived = lax.all_to_all(packed, "row", split_axis=0, concat_axis=0, tiled=True)
    mine = pl.pallas_call(
        functools.partial(compact_kernel, panel),
        out_shape=sds((cell, body, wide), F32),
        in_specs=[vspec()],
        out_specs=vspec(),
        name="compact",
    )(arrived)

    def turn(axis, count, by):
        return [(i, (i + by) % count) for i in range(count)]

    lefts = [mine] + [lax.ppermute(mine, "col", turn("col", cols_axis, -o)) for o in range(1, cols_axis)]
    lefts = [x.reshape(cell * parts, half, wide) for x in lefts]

    pair_list, starts = pl.pallas_call(
        pairs_kernel,
        out_shape=(
            sds((panel * parts * terms + DEPTH + 2 * GROUP,), jnp.int32),
            sds((8,), jnp.int32),
        ),
        in_specs=[sspec()] * 3,
        out_specs=(sspec(), sspec()),
        scratch_shapes=[SMEM((inner,), jnp.int32)],
        name="pairs",
    )(left_cols.T, right_cols.T, kept_cols.T)

    blocks = cell * kept

    def products(spec):
        def kernel(list_ref, start_ref, *refs):
            n_out = sum(len(ranges) for _, ranges in spec)
            outs = list(refs[5 : 5 + n_out])
            chunks = []
            for t, ranges in spec:
                chunks.append((t, [(outs.pop(0), lohi) for lohi in ranges]))
            product_kernel(chunks, list_ref, start_ref, *refs)

        shapes = tuple(sds((hi - lo, half, wide), F32) for _, ranges in spec for lo, hi in ranges)
        return pl.pallas_call(
            kernel,
            out_shape=shapes,
            in_specs=[sspec(), sspec()] + [aspec()] * 5,
            out_specs=tuple(vspec() for _ in shapes),
            scratch_shapes=[
                VMEM((panel * parts, half, wide), F32),
                VMEM((DEPTH, half, wide), F32),
                pltpu.SemaphoreType.DMA((4,)),
                pltpu.SemaphoreType.DMA((DEPTH,)),
            ],
            name="products",
        )(pair_list, starts, *lefts, right_all)

    mid = blocks // 2
    lower, upper = (0, mid), (mid, blocks)
    up, down = turn("layer", layers, 1), turn("layer", layers, -1)
    far_a, far_b = products([(0, [lower, upper])])
    got_a = lax.ppermute(far_a, "layer", up)
    got_b = lax.ppermute(far_b, "layer", down)
    one_a, one_b, three_a, three_b, own = products(
        [(1, [lower, upper]), (2, [lower, upper]), (3, [(0, blocks)])]
    )
    from_low_b = lax.ppermute(one_b, "layer", up)
    from_high_a = lax.ppermute(three_a, "layer", down)
    from_low_a = lax.ppermute(one_a + got_a, "layer", up)
    from_high_b = lax.ppermute(three_b + got_b, "layer", down)
    return pl.pallas_call(
        final_kernel,
        out_shape=sds((cell, kept, size, size), F32),
        in_specs=[vspec()] * 5,
        out_specs=vspec(),
        name="final",
    )(own, from_low_a, from_low_b, from_high_a, from_high_b)


def solution(mesh):
    placed = (
        P(("row", "col"), "layer", None, None),
        P(("row", "col")),
        P("row", "layer"),
        P(("layer", "row"), "col", None, None),
        P("layer", "col"),
        P("row", "col"),
    )
    return jax.shard_map(
        shards,
        mesh=mesh,
        in_specs=placed,
        out_specs=P(("row", "layer"), "col", None, None),
        check_vma=False,
    )
```

```python
import functools

import jax
import jax.numpy as jnp
from jax import lax
from jax.experimental import pallas as pl
from jax.experimental.pallas import tpu as pltpu
from jax.sharding import PartitionSpec as P

VMEM = pltpu.VMEM
SMEM = pltpu.SMEM
GROUP = 4
DEPTH = 16
CHUNKS = (2, 1, 3, 0)
F32 = jnp.float32
BF16 = jnp.bfloat16


def vspec():
    return pl.BlockSpec(memory_space=VMEM)


def sspec():
    return pl.BlockSpec(memory_space=SMEM)


def aspec():
    return pl.BlockSpec(memory_space=pl.ANY)


def limit(mib):
    return pltpu.CompilerParams(vmem_limit_bytes=mib << 20)


def folded(block):
    half = block.shape[0] // 2
    return jnp.concatenate([block[:half], block[half:]], axis=1)


def pack_right_kernel(blocks_ref, out_ref):
    rows, slots = blocks_ref.shape[:2]
    for i in range(rows):
        for k in range(slots):
            out_ref[i * slots + k] = folded(blocks_ref[i, k])


def pack_left_kernel(span, owned_ref, blocks_ref, *refs):
    out_refs, slot_of = refs[:-1], refs[-1]
    slots, parts, size = blocks_ref.shape[:3]
    chips = len(out_refs)
    groups = slot_of.shape[0]
    half = size // 2
    body = parts * half
    chip = lax.div(lax.axis_index("row"), 2)

    for g in range(groups):
        slot_of[g] = -1

    def find(s, carry):
        row = owned_ref[s]

        @pl.when(row >= 0)
        def _():
            slot_of[lax.div(row, span)] = s

        return carry

    lax.fori_loop(0, slots, find, 0)
    for d in range(chips):
        to = lax.rem(chip + d, chips) * 2
        for core in range(2):
            slot = slot_of[to + core]
            at = jnp.maximum(slot, 0)
            number = jnp.where(slot >= 0, owned_ref[at], -1).astype(F32)
            out_refs[d][core, body:, :] = jnp.full((out_refs[d].shape[1] - body, 2 * size), number, F32)
            for k in range(parts):
                out_refs[d][core, k * half : (k + 1) * half, :] = folded(blocks_ref[at, k])


def compact_kernel(span, *refs):
    arrived, (own_ref, other_ref) = refs[:-2], refs[-2:]
    cell, body = own_ref.shape[:2]
    row = lax.axis_index("row")
    core = lax.rem(row, 2)
    sides = ((own_ref, core, row), (other_ref, 1 - core, row + 1 - 2 * core))
    numbers = [
        [jnp.max(ref[side, body:, :]).astype(jnp.int32) for ref in arrived] for _, side, _ in sides
    ]
    own_ref[...] = jnp.zeros_like(own_ref)
    other_ref[...] = jnp.zeros_like(other_ref)
    for (out_ref, side, to), found in zip(sides, numbers):
        first = to * span + lax.axis_index("col") * cell
        for ref, number in zip(arrived, found):

            @pl.when(number >= 0)
            def _(out_ref=out_ref, side=side, first=first, ref=ref, number=number):
                out_ref[number - first] = ref[side, :body, :]


def join_kernel(mine_ref, other_ref, out_ref):
    count = mine_ref.shape[0]
    core = lax.rem(lax.axis_index("row"), 2)
    out_ref[pl.ds(core * count, count)] = mine_ref[...]
    out_ref[pl.ds((1 - core) * count, count)] = other_ref[...]


def pairs_kernel(chips, left_ref, right_ref, kept_ref, list_ref, start_ref, table):
    parts, rows = left_ref.shape
    terms, inner = right_ref.shape
    kept = kept_ref.shape[0]
    layers = len(CHUNKS)
    cell = rows // layers
    layer = lax.axis_index("layer")
    left_first = layer * inner
    per_device = inner // (2 * chips)
    chip = lax.div(lax.axis_index("row"), 2)
    core = lax.rem(lax.axis_index("row"), 2)
    right_first = lax.axis_index("col") * table.shape[0]

    def clear(i, carry):
        table[i] = -1
        return carry

    lax.fori_loop(0, table.shape[0], clear, 0)
    count = 0
    for t, distance in enumerate(CHUNKS):
        start_ref[t] = count
        base = lax.rem(layer + distance, layers) * cell

        def one_row(p, count, base=base):
            r = base + p
            for q in range(kept):
                table[kept_ref[q, r] - right_first] = q
            for k in range(parts):
                j = left_ref[k, r] - left_first
                source = lax.div(j, per_device)
                away = lax.rem(lax.div(source, 2) - chip + chips, chips)
                near = away <= chips // 2
                hops = jnp.where(near, away, chips - away)
                swapped = (hops > 0) & (near == (core == 0))
                held = hops + jnp.where(swapped, chips // 2, 0)
                first_block = (lax.rem(source, 2) * per_device + lax.rem(j, per_device)) * terms
                base_code = (r * parts + k) + held * 128 + first_block * 2048
                for l in range(terms):
                    q = table[right_ref[l, j] - right_first]
                    code = base_code + l * 2048 + (p * kept + q) * 131072
                    list_ref[count] = code
                    count = count + (q >= 0).astype(jnp.int32)
            for q in range(kept):
                table[kept_ref[q, r] - right_first] = -1
            return count

        count = lax.fori_loop(0, cell, one_row, count)
    start_ref[layers] = count
    for i in range(DEPTH + GROUP):
        list_ref[count + i] = 0


def product_kernel(chunks, n_right, list_ref, start_ref, *refs):
    left_refs, right_refs = refs[:4], refs[4 : 4 + n_right]
    out_refs = refs[4 + n_right : -4]
    left, ring, left_sems, ring_sems = refs[-4:]
    first, last = chunks[0][0], chunks[-1][0]
    per_source = left_refs[0].shape[0]
    col = lax.axis_index("col")
    copies = []
    for o in range(4):
        at = lax.rem(col + o, 4) * per_source
        copies.append(pltpu.make_async_copy(left_refs[o], left.at[pl.ds(at, per_source)], left_sems.at[o]))
        copies[-1].start()
    begin = start_ref[first]
    end = start_ref[last + 1]

    def field(code, shift, bits):
        return lax.shift_right_logical(code, shift) & ((1 << bits) - 1)

    def copy_of(ref, block, i):
        slot = lax.rem(i, DEPTH)
        return pltpu.make_async_copy(ref.at[block], ring.at[slot], ring_sems.at[slot])

    def fetch(i):
        code = list_ref[i]
        held, block = field(code, 7, 4), field(code, 11, 6)

        def choose(lo, hi):
            if hi - lo == 1:
                copy_of(right_refs[lo], block, i).start()
                return
            mid = (lo + hi) // 2

            @pl.when(held < mid)
            def _():
                choose(lo, mid)

            @pl.when(held >= mid)
            def _():
                choose(mid, hi)

        choose(0, n_right)

    def prime(i, carry):
        fetch(i)
        return carry

    lax.fori_loop(begin, jnp.minimum(begin + DEPTH, end), prime, 0)
    for _, targets in chunks:
        for ref, _ in targets:
            ref[...] = jnp.zeros_like(ref)
    for copy in copies:
        copy.wait()
    lane = lax.broadcasted_iota(jnp.int32, (32, 128), 1)
    low = lane < 64

    def product(i):
        code = list_ref[i]
        a = left[field(code, 0, 7)]
        b = ring[lax.rem(i, DEPTH)]
        turned = pltpu.roll(b, 64, 1)
        wide = jnp.concatenate(
            [
                jnp.where(low, b, 0.0),
                jnp.where(low, turned, 0.0),
                jnp.where(low, 0.0, turned),
                jnp.where(low, 0.0, b),
            ],
            axis=0,
        )
        a_hi = a.astype(BF16)
        a_lo = (a - a_hi.astype(F32)).astype(BF16)
        w_hi = wide.astype(BF16)
        w_lo = (wide - w_hi.astype(F32)).astype(BF16)
        main = jnp.dot(a_hi, w_hi, preferred_element_type=F32)
        rest = jnp.dot(a_lo, w_hi, preferred_element_type=F32) + jnp.dot(
            a_hi, w_lo, preferred_element_type=F32
        )
        return main + rest

    for t, targets in chunks:
        stop = start_ref[t + 1]
        start = start_ref[t]

        def group(g, carry, stop=stop, start=start, targets=targets):
            base = start + g * GROUP
            for u in range(GROUP):

                @pl.when(base + u < stop)
                def _(u=u):
                    copy_of(right_refs[0], 0, base + u).wait()

            values = [product(jnp.minimum(base + u, stop - 1)) for u in range(GROUP)]
            for u in range(GROUP):

                @pl.when((base + u < stop) & (base + u + DEPTH < end))
                def _(u=u):
                    fetch(base + u + DEPTH)

            for u in range(GROUP):
                spot = field(list_ref[base + u], 17, 6)
                for ref, (lo, hi) in targets:

                    @pl.when((base + u < stop) & (spot >= lo) & (spot < hi))
                    def _(u=u, ref=ref, lo=lo, spot=spot):
                        ref[spot - lo] += values[u]

            return carry

        lax.fori_loop(0, lax.div(stop - start + GROUP - 1, GROUP), group, 0)


def final_kernel(own_ref, a0, a1, b0, b1, out_ref):
    rows, kept, size = out_ref.shape[:3]
    half = size // 2
    per = a0.shape[0]

    for i in range(rows * kept):
        p, q = i // kept, i % kept
        x, y = (a0, b0) if i < per else (a1, b1)
        total = own_ref[i] + x[i % per] + y[i % per]
        out_ref[p, q, :half, :] = total[:, :size]
        out_ref[p, q, half:, :] = total[:, size:]


def shards(ks_owned, owned_rows, left_cols, right_blocks, right_cols, kept_cols):
    rows_axis = lax.axis_size("row")
    cols_axis = lax.axis_size("col")
    layers = lax.axis_size("layer")
    slots, parts, size = ks_owned.shape[:3]
    half, wide = size // 2, size * 2
    panel = left_cols.shape[0]
    cell = panel // cols_axis
    inner, terms = right_cols.shape
    kept = kept_cols.shape[1]
    body = parts * half
    sds = jax.ShapeDtypeStruct

    chips = rows_axis // 2

    def turn(count, by):
        return [(i, (i + by) % count) for i in range(count)]

    def along(by):
        return [(i, (i + 2 * by) % rows_axis) for i in range(rows_axis)]

    swap = [(i, i ^ 1) for i in range(rows_axis)]
    both = [(i, (i + (-2 if i % 2 else 2)) % rows_axis) for i in range(rows_axis)]
    down_only = [pair for pair in both if pair[0] % 2]
    to_even = [(i, i - 1) for i in range(1, rows_axis, 2)]

    packed = pl.pallas_call(
        functools.partial(pack_left_kernel, panel),
        out_shape=(sds((2, body + 8, wide), F32),) * chips,
        in_specs=[sspec(), vspec()],
        out_specs=(vspec(),) * chips,
        scratch_shapes=[SMEM((rows_axis,), jnp.int32)],
        compiler_params=limit(8),
        name="pack_left",
    )(owned_rows, ks_owned)
    arrived = [packed[0]] + [None] * (chips - 1)
    for d in (4, 3, 5, 2, 6, 1, 7):
        arrived[d] = lax.ppermute(packed[d], "row", along(d))

    right = pl.pallas_call(
        pack_right_kernel,
        out_shape=sds((right_blocks.shape[0] * terms, half, wide), F32),
        in_specs=[vspec()],
        out_specs=vspec(),
        compiler_params=limit(4),
        name="pack_right",
    )(right_blocks)
    joined = pl.pallas_call(
        join_kernel,
        out_shape=sds((2 * right.shape[0], half, wide), F32),
        in_specs=[vspec(), vspec()],
        out_specs=vspec(),
        compiler_params=limit(4),
        name="join",
    )(right, lax.ppermute(right, "row", swap))
    straight, swapped = [joined], []
    for hop in range(1, chips // 2 + 1):
        last = hop == chips // 2
        straight.append(lax.ppermute(straight[-1], "row", down_only if last else both))
        swapped.append(lax.ppermute(straight[-1], "row", to_even if last else swap))
    rights = straight + swapped

    own_rows, other_rows = pl.pallas_call(
        functools.partial(compact_kernel, panel),
        out_shape=(sds((cell, body, wide), F32),) * 2,
        in_specs=[vspec()] * chips,
        out_specs=(vspec(), vspec()),
        compiler_params=limit(6),
        name="compact",
    )(*arrived)
    mine = own_rows + lax.ppermute(other_rows, "row", swap)

    lefts = [mine] + [lax.ppermute(mine, "col", turn(cols_axis, -o)) for o in range(1, cols_axis)]
    lefts = [x.reshape(cell * parts, half, wide) for x in lefts]

    pair_list, starts = pl.pallas_call(
        functools.partial(pairs_kernel, chips),
        out_shape=(
            sds((panel * parts * terms + DEPTH + 2 * GROUP,), jnp.int32),
            sds((8,), jnp.int32),
        ),
        in_specs=[sspec()] * 3,
        out_specs=(sspec(), sspec()),
        scratch_shapes=[SMEM((inner,), jnp.int32)],
        name="pairs",
    )(left_cols.T, right_cols.T, kept_cols.T)

    blocks = cell * kept

    def products(spec):
        def kernel(list_ref, start_ref, *refs):
            n_out = sum(len(ranges) for _, ranges in spec)
            outs = list(refs[4 + len(rights) : 4 + len(rights) + n_out])
            chunks = []
            for t, ranges in spec:
                chunks.append((t, [(outs.pop(0), lohi) for lohi in ranges]))
            product_kernel(chunks, len(rights), list_ref, start_ref, *refs)

        shapes = tuple(sds((hi - lo, half, wide), F32) for _, ranges in spec for lo, hi in ranges)
        return pl.pallas_call(
            kernel,
            out_shape=shapes,
            in_specs=[sspec(), sspec()] + [aspec()] * (4 + len(rights)),
            out_specs=tuple(vspec() for _ in shapes),
            scratch_shapes=[
                VMEM((panel * parts, half, wide), F32),
                VMEM((DEPTH, half, wide), F32),
                pltpu.SemaphoreType.DMA((4,)),
                pltpu.SemaphoreType.DMA((DEPTH,)),
            ],
            compiler_params=limit(8),
            name="products",
        )(pair_list, starts, *lefts, *rights)

    mid = blocks // 2
    lower, upper = (0, mid), (mid, blocks)
    up, down = turn(layers, 1), turn(layers, -1)
    far_a, far_b = products([(0, [lower, upper])])
    got_a = lax.ppermute(far_a, "layer", up)
    got_b = lax.ppermute(far_b, "layer", down)
    one_a, one_b, three_a, three_b, own = products(
        [(1, [lower, upper]), (2, [lower, upper]), (3, [(0, blocks)])]
    )
    from_low_b = lax.ppermute(one_b, "layer", up)
    from_high_a = lax.ppermute(three_a, "layer", down)
    from_low_a = lax.ppermute(one_a + got_a, "layer", up)
    from_high_b = lax.ppermute(three_b + got_b, "layer", down)
    return pl.pallas_call(
        final_kernel,
        out_shape=sds((cell, kept, size, size), F32),
        in_specs=[vspec()] * 5,
        out_specs=vspec(),
        compiler_params=limit(8),
        name="final",
    )(own, from_low_a, from_low_b, from_high_a, from_high_b)


def solution(mesh):
    placed = (
        P(("row", "col"), "layer", None, None),
        P(("row", "col")),
        P("row", "layer"),
        P(("layer", "row"), "col", None, None),
        P("layer", "col"),
        P("row", "col"),
    )
    return jax.shard_map(
        shards,
        mesh=mesh,
        in_specs=placed,
        out_specs=P(("row", "layer"), "col", None, None),
        check_vma=False,
    )
```

```python
import functools

import jax
import jax.numpy as jnp
from jax import lax
from jax.experimental import pallas as pl
from jax.experimental.pallas import tpu as pltpu
from jax.sharding import PartitionSpec as P

VMEM = pltpu.VMEM
SMEM = pltpu.SMEM
GROUP = 4
DEPTH = 16
CHUNKS = (2, 1, 3, 0)
F32 = jnp.float32
BF16 = jnp.bfloat16


def vspec():
    return pl.BlockSpec(memory_space=VMEM)


def sspec():
    return pl.BlockSpec(memory_space=SMEM)


def aspec():
    return pl.BlockSpec(memory_space=pl.ANY)


def limit(mib):
    return pltpu.CompilerParams(vmem_limit_bytes=mib << 20)


def folded(block):
    half = block.shape[0] // 2
    return jnp.concatenate([block[:half], block[half:]], axis=1)


def pack_right_kernel(blocks_ref, out_ref):
    rows, slots = blocks_ref.shape[:2]
    for i in range(rows):
        for k in range(slots):
            out_ref[i * slots + k] = folded(blocks_ref[i, k])


def pack_left_kernel(span, owned_ref, blocks_ref, self_ref, keep_ref, give_ref, slot_of):
    slots, parts, size = blocks_ref.shape[:3]
    groups = slot_of.shape[0]
    chips = groups // 2
    half = size // 2
    body = parts * half
    row = lax.axis_index("row")
    chip, core = lax.div(row, 2), lax.rem(row, 2)

    for g in range(groups):
        slot_of[g] = -1

    def find(s, carry):
        row = owned_ref[s]

        @pl.when(row >= 0)
        def _():
            slot_of[lax.div(row, span)] = s

        return carry

    lax.fori_loop(0, slots, find, 0)

    def put(out_ref, n, to_chip, to_core):
        slot = slot_of[to_chip * 2 + to_core]
        at = jnp.maximum(slot, 0)
        number = jnp.where(slot >= 0, owned_ref[at], -1).astype(F32)
        out_ref[n, body:, :] = jnp.full((out_ref.shape[1] - body, 2 * size), number, F32)
        for k in range(parts):
            out_ref[n, k * half : (k + 1) * half, :] = folded(blocks_ref[at, k])

    for out_ref, carrier in ((give_ref, 1 - core), (keep_ref, core)):
        for hop in range(1, chips // 2):
            to_chip = lax.rem(chip + chips + hop - 2 * hop * carrier, chips)
            put(out_ref, 2 * hop - 2, to_chip, 0)
            put(out_ref, 2 * hop - 1, to_chip, 1)
        put(out_ref, chips - 2, lax.rem(chip + chips // 2, chips), carrier)
    put(self_ref, 0, chip, 0)
    put(self_ref, 1, chip, 1)


def join_left_kernel(keep_ref, got_ref, after_ref, *out_refs):
    at = 0
    for ref in out_refs:
        count = ref.shape[0] // 2
        ref[:count] = keep_ref[at : at + count]
        ref[count:] = got_ref[at : at + count]
        at += count


def join_kernel(first_ref, second_ref, out_ref):
    count = first_ref.shape[0]
    out_ref[:count] = first_ref[...]
    out_ref[count:] = second_ref[...]


def compact_kernel(span, *refs):
    arrived, (own_ref, other_ref) = refs[:-3], refs[-2:]
    cell, body = own_ref.shape[:2]
    row = lax.axis_index("row")
    core = lax.rem(row, 2)
    own = [(arrived[0], core)] + [(ref, n + core) for ref in arrived[1:-1] for n in (0, 2)]
    own += [(arrived[-1], 0), (arrived[-1], 1)]
    other = [(arrived[0], 1 - core)] + [(ref, n + 1 - core) for ref in arrived[1:-1] for n in (0, 2)]
    sides = ((own_ref, own, row), (other_ref, other, row + 1 - 2 * core))
    numbers = [[jnp.max(ref[n, body:, :]).astype(jnp.int32) for ref, n in side] for _, side, _ in sides]
    own_ref[...] = jnp.zeros_like(own_ref)
    other_ref[...] = jnp.zeros_like(other_ref)
    for (out_ref, side, to), found in zip(sides, numbers):
        first = to * span + lax.axis_index("col") * cell
        for (ref, n), number in zip(side, found):

            @pl.when(number >= 0)
            def _(out_ref=out_ref, first=first, ref=ref, n=n, number=number):
                out_ref[number - first] = ref[n, :body, :]


def gate(array, *after):
    return pl.pallas_call(
        lambda *refs: None,
        out_shape=jax.ShapeDtypeStruct(array.shape, array.dtype),
        in_specs=[aspec()] * (1 + len(after)),
        out_specs=aspec(),
        input_output_aliases={0: 0},
        compiler_params=limit(1),
        name="gate",
    )(array, *after)


def pairs_kernel(chips, left_ref, right_ref, kept_ref, list_ref, table):
    parts, rows = left_ref.shape
    terms, inner = right_ref.shape
    kept = kept_ref.shape[0]
    layers = len(CHUNKS)
    cell = rows // layers
    layer = lax.axis_index("layer")
    left_first = layer * inner
    per_device = inner // (2 * chips)
    chip = lax.div(lax.axis_index("row"), 2)
    core = lax.rem(lax.axis_index("row"), 2)
    right_first = lax.axis_index("col") * table.shape[0]

    def clear(i, carry):
        table[i] = -1
        return carry

    lax.fori_loop(0, table.shape[0], clear, 0)
    count = 0
    for t, distance in enumerate(CHUNKS):
        list_ref[list_ref.shape[0] - 8 + t] = count
        base = lax.rem(layer + distance, layers) * cell

        def one_row(p, count, base=base):
            r = base + p
            for q in range(kept):
                table[kept_ref[q, r] - right_first] = q
            for k in range(parts):
                j = left_ref[k, r] - left_first
                source = lax.div(j, per_device)
                of_core = lax.rem(source, 2)
                away = lax.rem(lax.div(source, 2) - chip + chips, chips)
                ahead = jnp.where(away * 2 == chips, of_core, (away * 2 < chips).astype(jnp.int32))
                hops = jnp.where(away * 2 <= chips, away, chips - away)
                far = chips // 2
                held = 1 + hops
                second = (ahead != of_core).astype(jnp.int32)
                crossed = (ahead != core).astype(jnp.int32)
                held = held + jnp.where(crossed == 1, 2 * far - 1, far * second)
                held = jnp.where(hops == 0, jnp.where(of_core == core, 0, 1), held)
                first_block = (crossed * second * per_device + lax.rem(j, per_device)) * terms
                first_block = jnp.where(hops == 0, lax.rem(j, per_device) * terms, first_block)
                base_code = (r * parts + k) + held * 128 + first_block * 2048
                for l in range(terms):
                    q = table[right_ref[l, j] - right_first]
                    code = base_code + l * 2048 + (p * kept + q) * 131072
                    list_ref[count] = code
                    count = count + (q >= 0).astype(jnp.int32)
            for q in range(kept):
                table[kept_ref[q, r] - right_first] = -1
            return count

        count = lax.fori_loop(0, cell, one_row, count)
    list_ref[list_ref.shape[0] - 8 + layers] = count
    for i in range(DEPTH + GROUP):
        list_ref[count + i] = 0


def product_kernel(chunks, places, n_right, list_ref, *refs):
    left_refs, right_refs = refs[: len(places)], refs[len(places) : len(places) + n_right]
    left, ring, left_sems, ring_sems = refs[-4:]

    def start_of(t):
        return list_ref[list_ref.shape[0] - 8 + t]

    first, last = chunks[0][0], chunks[-1][0]
    per_source = left_refs[0].shape[0]
    col = lax.axis_index("col")
    copies = []
    for n, (further, first_row) in enumerate(places):
        at = lax.rem(col + further, 4) * per_source + first_row
        count = left_refs[n].shape[0]
        copies.append(pltpu.make_async_copy(left_refs[n], left.at[pl.ds(at, count)], left_sems.at[n]))
        copies[-1].start()
    begin = start_of(first)
    end = start_of(last + 1)

    def field(code, shift, bits):
        return lax.shift_right_logical(code, shift) & ((1 << bits) - 1)

    def copy_of(ref, block, i):
        slot = lax.rem(i, DEPTH)
        return pltpu.make_async_copy(ref.at[block], ring.at[slot], ring_sems.at[slot])

    def fetch(i):
        code = list_ref[i]
        held, block = field(code, 7, 4), field(code, 11, 6)

        def choose(lo, hi):
            if hi - lo == 1:
                copy_of(right_refs[lo], block, i).start()
                return
            mid = (lo + hi) // 2

            @pl.when(held < mid)
            def _():
                choose(lo, mid)

            @pl.when(held >= mid)
            def _():
                choose(mid, hi)

        choose(0, n_right)

    def prime(i, carry):
        fetch(i)
        return carry

    lax.fori_loop(begin, jnp.minimum(begin + DEPTH, end), prime, 0)
    for _, targets in chunks:
        for ref, _ in targets:
            ref[...] = jnp.zeros_like(ref)
    for copy in copies:
        copy.wait()
    lane = lax.broadcasted_iota(jnp.int32, (32, 128), 1)
    low = lane < 64

    def product(i):
        code = list_ref[i]
        a = left[field(code, 0, 7)]
        b = ring[lax.rem(i, DEPTH)]
        turned = pltpu.roll(b, 64, 1)
        wide = jnp.concatenate(
            [
                jnp.where(low, b, 0.0),
                jnp.where(low, turned, 0.0),
                jnp.where(low, 0.0, turned),
                jnp.where(low, 0.0, b),
            ],
            axis=0,
        )
        a_hi = a.astype(BF16)
        a_lo = (a - a_hi.astype(F32)).astype(BF16)
        w_hi = wide.astype(BF16)
        w_lo = (wide - w_hi.astype(F32)).astype(BF16)
        main = jnp.dot(a_hi, w_hi, preferred_element_type=F32)
        rest = jnp.dot(a_lo, w_hi, preferred_element_type=F32) + jnp.dot(
            a_hi, w_lo, preferred_element_type=F32
        )
        return main + rest

    for t, targets in chunks:
        stop = start_of(t + 1)
        start = start_of(t)

        def group(g, carry, stop=stop, start=start, targets=targets):
            base = start + g * GROUP
            for u in range(GROUP):

                @pl.when(base + u < stop)
                def _(u=u):
                    copy_of(right_refs[0], 0, base + u).wait()

            values = [product(jnp.minimum(base + u, stop - 1)) for u in range(GROUP)]
            for u in range(GROUP):

                @pl.when((base + u < stop) & (base + u + DEPTH < end))
                def _(u=u):
                    fetch(base + u + DEPTH)

            for u in range(GROUP):
                spot = field(list_ref[base + u], 17, 6)
                for ref, (lo, hi) in targets:

                    @pl.when((base + u < stop) & (spot >= lo) & (spot < hi))
                    def _(u=u, ref=ref, lo=lo, spot=spot):
                        ref[spot - lo] += values[u]

            return carry

        lax.fori_loop(0, lax.div(stop - start + GROUP - 1, GROUP), group, 0)


def final_kernel(own_ref, a0, a1, b0, b1, out_ref):
    rows, kept, size = out_ref.shape[:3]
    half = size // 2
    per = a0.shape[0]

    for i in range(rows * kept):
        p, q = i // kept, i % kept
        x, y = (a0, b0) if i < per else (a1, b1)
        total = own_ref[i] + x[i % per] + y[i % per]
        out_ref[p, q, :half, :] = total[:, :size]
        out_ref[p, q, half:, :] = total[:, size:]


def shards(ks_owned, owned_rows, left_cols, right_blocks, right_cols, kept_cols):
    rows_axis = lax.axis_size("row")
    cols_axis = lax.axis_size("col")
    layers = lax.axis_size("layer")
    slots, parts, size = ks_owned.shape[:3]
    half, wide = size // 2, size * 2
    panel = left_cols.shape[0]
    cell = panel // cols_axis
    inner, terms = right_cols.shape
    kept = kept_cols.shape[1]
    body = parts * half
    sds = jax.ShapeDtypeStruct

    chips = rows_axis // 2

    def turn(count, by):
        return [(i, (i + by) % count) for i in range(count)]

    def along(by):
        return [(i, (i + 2 * by) % rows_axis) for i in range(rows_axis)]

    swap = [(i, i ^ 1) for i in range(rows_axis)]
    def hops(by):
        return [(i, (i + (-2 if i % 2 else 2) * by) % rows_axis) for i in range(rows_axis)]

    def ring(x):
        return lax.ppermute(x, "row", hops(1))

    def swapped(x):
        return lax.ppermute(x, "row", swap)

    right = pl.pallas_call(
        pack_right_kernel,
        out_shape=sds((right_blocks.shape[0] * terms, half, wide), F32),
        in_specs=[vspec()],
        out_specs=vspec(),
        compiler_params=limit(4),
        name="pack_right",
    )(right_blocks)
    right_two = swapped(right)

    opposite = chips // 2
    self_rows, keep, give = pl.pallas_call(
        functools.partial(pack_left_kernel, panel),
        out_shape=(sds((2, body + 8, wide), F32),) + (sds((chips - 1, body + 8, wide), F32),) * 2,
        in_specs=[sspec(), vspec()],
        out_specs=(vspec(),) * 3,
        scratch_shapes=[SMEM((rows_axis,), jnp.int32)],
        compiler_params=limit(8),
        name="pack_left",
    )(owned_rows, ks_owned)
    sent = pl.pallas_call(
        join_left_kernel,
        out_shape=tuple(
            sds((2 if hop == opposite else 4, body + 8, wide), F32) for hop in range(1, opposite + 1)
        ),
        in_specs=[vspec()] * 2 + [aspec()],
        out_specs=(vspec(),) * opposite,
        compiler_params=limit(6),
        name="join_left",
    )(keep, swapped(give), right_two)
    arrived = [self_rows] + [None] * opposite
    for hop in range(opposite, 0, -1):
        arrived[hop] = lax.ppermute(sent[hop - 1], "row", hops(hop))

    list_size = panel * parts * terms + DEPTH + 2 * GROUP + 8
    pair_list = pl.pallas_call(
        functools.partial(pairs_kernel, chips),
        out_shape=sds((list_size,), jnp.int32),
        in_specs=[sspec()] * 3,
        out_specs=sspec(),
        scratch_shapes=[SMEM((inner,), jnp.int32)],
        compiler_params=limit(1),
        name="pairs",
    )(left_cols.T, right_cols.T, kept_cols.T)

    own_rows, other_rows = pl.pallas_call(
        functools.partial(compact_kernel, panel),
        out_shape=(sds((cell, body, wide), F32),) * 2,
        in_specs=[vspec()] * len(arrived) + [aspec()],
        out_specs=(vspec(), vspec()),
        compiler_params=limit(6),
        name="compact",
    )(*arrived, pair_list)
    mine = own_rows + lax.ppermute(other_rows, "row", swap)

    rows_of = cell * parts
    mine = mine.reshape(rows_of, half, wide)
    above = lax.ppermute(mine, "col", turn(cols_axis, -1))
    below = lax.ppermute(mine, "col", turn(cols_axis, 1))
    first_half = lax.ppermute(below[: rows_of // 2], "col", turn(cols_axis, 1))
    second_half = lax.ppermute(above[rows_of // 2 :], "col", turn(cols_axis, -1))
    lefts = [(mine, 0, 0), (above, 1, 0), (below, 3, 0), (first_half, 2, 0), (second_half, 2, rows_of // 2)]

    def joined(a, b):
        return pl.pallas_call(
            join_kernel,
            out_shape=sds((2 * a.shape[0],) + a.shape[1:], F32),
            in_specs=[vspec()] * 2,
            out_specs=vspec(),
            compiler_params=limit(4),
            name="join",
        )(a, b)

    a1, b1 = ring(right), ring(right_two)
    a2, b2 = ring(a1), ring(b1)
    a3, b3 = ring(a2), ring(b2)
    a4 = gate(ring(a3), first_half, second_half)
    rights = [right, right_two, a1, a2, a3, a4, b1, b2, b3]
    rights += [swapped(joined(a1, b1)), swapped(joined(a2, b2)), swapped(joined(a3, b3)), swapped(a4)]

    blocks = cell * kept

    def products(spec):
        def kernel(list_ref, *refs):
            n_out = sum(len(ranges) for _, ranges in spec)
            outs = list(refs[len(lefts) + len(rights) :][:n_out])
            chunks = []
            for t, ranges in spec:
                chunks.append((t, [(outs.pop(0), lohi) for lohi in ranges]))
            product_kernel(chunks, [place for _, *place in lefts], len(rights), list_ref, *refs)

        shapes = tuple(sds((hi - lo, half, wide), F32) for _, ranges in spec for lo, hi in ranges)
        return pl.pallas_call(
            kernel,
            out_shape=shapes,
            in_specs=[sspec()] + [aspec()] * (len(lefts) + len(rights)),
            out_specs=tuple(vspec() for _ in shapes),
            scratch_shapes=[
                VMEM((panel * parts, half, wide), F32),
                VMEM((DEPTH, half, wide), F32),
                pltpu.SemaphoreType.DMA((len(lefts),)),
                pltpu.SemaphoreType.DMA((DEPTH,)),
            ],
            compiler_params=limit(8),
            name="products",
        )(pair_list, *[x for x, _, _ in lefts], *rights)

    mid = blocks // 2
    lower, upper = (0, mid), (mid, blocks)
    up, down = turn(layers, 1), turn(layers, -1)
    far_a, far_b = products([(0, [lower, upper])])
    got_a = lax.ppermute(far_a, "layer", up)
    got_b = lax.ppermute(far_b, "layer", down)
    one_a, one_b, three_a, three_b, own = products(
        [(1, [lower, upper]), (2, [lower, upper]), (3, [(0, blocks)])]
    )
    from_low_b = lax.ppermute(one_b, "layer", up)
    from_high_a = lax.ppermute(three_a, "layer", down)
    from_low_a = lax.ppermute(one_a + got_a, "layer", up)
    from_high_b = lax.ppermute(three_b + got_b, "layer", down)
    return pl.pallas_call(
        final_kernel,
        out_shape=sds((cell, kept, size, size), F32),
        in_specs=[vspec()] * 5,
        out_specs=vspec(),
        compiler_params=limit(8),
        name="final",
    )(own, from_low_a, from_low_b, from_high_a, from_high_b)


def solution(mesh):
    placed = (
        P(("row", "col"), "layer", None, None),
        P(("row", "col")),
        P("row", "layer"),
        P(("layer", "row"), "col", None, None),
        P("layer", "col"),
        P("row", "col"),
    )
    return jax.shard_map(
        shards,
        mesh=mesh,
        in_specs=placed,
        out_specs=P(("row", "layer"), "col", None, None),
        check_vma=False,
    )
```

```python
import functools

import jax
import jax.numpy as jnp
from jax import lax
from jax.experimental import pallas as pl
from jax.experimental.pallas import tpu as pltpu
from jax.sharding import PartitionSpec as P

VMEM = pltpu.VMEM
SMEM = pltpu.SMEM
GROUP = 4
CHUNKS = (2, 1, 3, 0)
F32 = jnp.float32
BF16 = jnp.bfloat16


def vspec():
    return pl.BlockSpec(memory_space=VMEM)


def sspec():
    return pl.BlockSpec(memory_space=SMEM)


def aspec():
    return pl.BlockSpec(memory_space=pl.ANY)


def limit(mib):
    return pltpu.CompilerParams(vmem_limit_bytes=mib << 20)


def folded(block):
    half = block.shape[0] // 2
    return jnp.concatenate([block[:half], block[half:]], axis=1)


def pack_right_kernel(blocks_ref, out_ref):
    rows, slots = blocks_ref.shape[:2]
    for i in range(rows):
        for k in range(slots):
            out_ref[i * slots + k] = folded(blocks_ref[i, k])


def pack_left_kernel(span, owned_ref, blocks_ref, self_ref, keep_ref, give_ref, slot_of):
    slots, parts, size = blocks_ref.shape[:3]
    groups = slot_of.shape[0]
    chips = groups // 2
    half = size // 2
    body = parts * half
    row = lax.axis_index("row")
    chip, core = lax.div(row, 2), lax.rem(row, 2)

    for g in range(groups):
        slot_of[g] = -1

    def find(s, carry):
        row = owned_ref[s]

        @pl.when(row >= 0)
        def _():
            slot_of[lax.div(row, span)] = s

        return carry

    lax.fori_loop(0, slots, find, 0)

    def put(out_ref, n, to_chip, to_core):
        slot = slot_of[to_chip * 2 + to_core]
        at = jnp.maximum(slot, 0)
        number = jnp.where(slot >= 0, owned_ref[at], -1).astype(F32)
        out_ref[n, body:, :] = jnp.full((out_ref.shape[1] - body, 2 * size), number, F32)
        for k in range(parts):
            out_ref[n, k * half : (k + 1) * half, :] = folded(blocks_ref[at, k])

    for out_ref, carrier in ((give_ref, 1 - core), (keep_ref, core)):
        for hop in range(1, chips // 2):
            to_chip = lax.rem(chip + chips + hop - 2 * hop * carrier, chips)
            put(out_ref, 2 * hop - 2, to_chip, 0)
            put(out_ref, 2 * hop - 1, to_chip, 1)
        put(out_ref, chips - 2, lax.rem(chip + chips // 2, chips), carrier)
    put(self_ref, 0, chip, 0)
    put(self_ref, 1, chip, 1)


def join_left_kernel(keep_ref, got_ref, after_ref, *out_refs):
    at = 0
    for ref in out_refs:
        count = ref.shape[0] // 2
        ref[:count] = keep_ref[at : at + count]
        ref[count:] = got_ref[at : at + count]
        at += count


def join_kernel(first_ref, second_ref, out_ref):
    count = first_ref.shape[0]
    out_ref[:count] = first_ref[...]
    out_ref[count:] = second_ref[...]


def compact_kernel(span, *refs):
    arrived, (own_ref, other_ref) = refs[:-3], refs[-2:]
    cell, body = own_ref.shape[:2]
    row = lax.axis_index("row")
    core = lax.rem(row, 2)
    own = [(arrived[0], core)] + [(ref, n + core) for ref in arrived[1:-1] for n in (0, 2)]
    own += [(arrived[-1], 0), (arrived[-1], 1)]
    other = [(arrived[0], 1 - core)] + [(ref, n + 1 - core) for ref in arrived[1:-1] for n in (0, 2)]
    sides = ((own_ref, own, row), (other_ref, other, row + 1 - 2 * core))
    numbers = [[jnp.max(ref[n, body:, :]).astype(jnp.int32) for ref, n in side] for _, side, _ in sides]
    own_ref[...] = jnp.zeros_like(own_ref)
    other_ref[...] = jnp.zeros_like(other_ref)
    for (out_ref, side, to), found in zip(sides, numbers):
        first = to * span + lax.axis_index("col") * cell
        for (ref, n), number in zip(side, found):

            @pl.when(number >= 0)
            def _(out_ref=out_ref, first=first, ref=ref, n=n, number=number):
                out_ref[number - first] = ref[n, :body, :]


def gate(array, *after, flops=0):
    return pl.pallas_call(
        lambda *refs: None,
        out_shape=jax.ShapeDtypeStruct(array.shape, array.dtype),
        in_specs=[aspec()] * (1 + len(after)),
        out_specs=aspec(),
        input_output_aliases={0: 0},
        compiler_params=limit(1),
        cost_estimate=pl.CostEstimate(flops=flops, bytes_accessed=0, transcendentals=0),
        name="gate",
    )(array, *after)


def pairs_kernel(chips, left_ref, right_ref, kept_ref, list_ref, table):
    parts, rows = left_ref.shape
    terms, inner = right_ref.shape
    kept = kept_ref.shape[0]
    layers = len(CHUNKS)
    cell = rows // layers
    layer = lax.axis_index("layer")
    left_first = layer * inner
    per_device = inner // (2 * chips)
    chip = lax.div(lax.axis_index("row"), 2)
    core = lax.rem(lax.axis_index("row"), 2)
    right_first = lax.axis_index("col") * table.shape[0]

    def clear(i, carry):
        table[i] = -1
        return carry

    lax.fori_loop(0, table.shape[0], clear, 0)
    count = 0
    for t, distance in enumerate(CHUNKS):
        list_ref[list_ref.shape[0] - 8 + t] = count
        base = lax.rem(layer + distance, layers) * cell

        def one_row(p, count, base=base):
            r = base + p
            for q in range(kept):
                table[kept_ref[q, r] - right_first] = q
            for k in range(parts):
                j = left_ref[k, r] - left_first
                source = lax.div(j, per_device)
                of_core = lax.rem(source, 2)
                away = lax.rem(lax.div(source, 2) - chip + chips, chips)
                ahead = jnp.where(away * 2 == chips, of_core, (away * 2 < chips).astype(jnp.int32))
                hops = jnp.where(away * 2 <= chips, away, chips - away)
                far = chips // 2
                held = 1 + hops
                second = (ahead != of_core).astype(jnp.int32)
                crossed = (ahead != core).astype(jnp.int32)
                held = held + jnp.where(crossed == 1, 2 * far - 1, far * second)
                held = jnp.where(hops == 0, jnp.where(of_core == core, 0, 1), held)
                first_block = (crossed * second * per_device + lax.rem(j, per_device)) * terms
                first_block = jnp.where(hops == 0, lax.rem(j, per_device) * terms, first_block)
                base_code = (r * parts + k) + held * 128 + first_block * 2048
                for l in range(terms):
                    q = table[right_ref[l, j] - right_first]
                    code = base_code + l * 2048 + (p * kept + q) * 131072
                    list_ref[count] = code
                    count = count + (q >= 0).astype(jnp.int32)
            for q in range(kept):
                table[kept_ref[q, r] - right_first] = -1
            return count

        count = lax.fori_loop(0, cell, one_row, count)
    list_ref[list_ref.shape[0] - 8 + layers] = count


def product_kernel(chunks, places, n_right, list_ref, *refs):
    left_refs, right_refs = refs[: len(places)], refs[len(places) : len(places) + n_right]
    left, ring = refs[-2:]
    layers = len(CHUNKS)
    per_source = left_refs[0].shape[0]
    col = lax.axis_index("col")

    def start_of(t):
        return list_ref[list_ref.shape[0] - 8 + t]

    def field(code, shift, bits):
        return lax.shift_right_logical(code, shift) & ((1 << bits) - 1)

    for n, (further, first_row) in enumerate(places):
        at = lax.rem(col + further, layers) * per_source + first_row
        left[pl.ds(at, left_refs[n].shape[0])] = left_refs[n][...]
    for _, targets in chunks:
        for ref, _ in targets:
            ref[...] = jnp.zeros_like(ref)

    def fetch(code, u):
        held, block = field(code, 7, 4), field(code, 11, 6)

        def choose(lo, hi):
            if hi - lo == 1:
                ring[u] = right_refs[lo][block]
                return
            mid = (lo + hi) // 2

            @pl.when(held < mid)
            def _():
                choose(lo, mid)

            @pl.when(held >= mid)
            def _():
                choose(mid, hi)

        choose(0, n_right)

    half, wide = ring.shape[1:]
    low = lax.broadcasted_iota(jnp.int32, (half, wide), 1) < half * 2

    def product(code, u):
        a = left[field(code, 0, 7)]
        b = ring[u]
        turned = pltpu.roll(b, wide // 2, 1)
        full = jnp.concatenate(
            [
                jnp.where(low, b, 0.0),
                jnp.where(low, turned, 0.0),
                jnp.where(low, 0.0, turned),
                jnp.where(low, 0.0, b),
            ],
            axis=0,
        )
        a_hi = a.astype(BF16)
        a_lo = (a - a_hi.astype(F32)).astype(BF16)
        f_hi = full.astype(BF16)
        f_lo = (full - f_hi.astype(F32)).astype(BF16)
        main = jnp.dot(a_hi, f_hi, preferred_element_type=F32)
        rest = jnp.dot(a_lo, f_hi, preferred_element_type=F32) + jnp.dot(
            a_hi, f_lo, preferred_element_type=F32
        )
        return main + rest

    for t, targets in chunks:
        start, stop = start_of(t), start_of(t + 1)

        def group(g, carry, start=start, stop=stop, targets=targets):
            base = start + g * GROUP
            codes = [list_ref[jnp.minimum(base + u, stop - 1)] for u in range(GROUP)]
            for u in range(GROUP):
                fetch(codes[u], u)
            values = [product(codes[u], u) for u in range(GROUP)]
            for u in range(GROUP):
                spot = field(codes[u], 17, 6)
                for ref, (lo, hi) in targets:

                    @pl.when((base + u < stop) & (spot >= lo) & (spot < hi))
                    def _(u=u, ref=ref, lo=lo, spot=spot):
                        ref[spot - lo] += values[u]

            return carry

        lax.fori_loop(0, lax.div(stop - start + GROUP - 1, GROUP), group, 0)


def final_kernel(own_ref, a0, a1, b0, b1, out_ref):
    rows, kept, size = out_ref.shape[:3]
    half = size // 2
    per = a0.shape[0]

    for i in range(rows * kept):
        p, q = i // kept, i % kept
        x, y = (a0, b0) if i < per else (a1, b1)
        total = own_ref[i] + x[i % per] + y[i % per]
        out_ref[p, q, :half, :] = total[:, :size]
        out_ref[p, q, half:, :] = total[:, size:]


def shards(ks_owned, owned_rows, left_cols, right_blocks, right_cols, kept_cols):
    rows_axis = lax.axis_size("row")
    cols_axis = lax.axis_size("col")
    layers = lax.axis_size("layer")
    slots, parts, size = ks_owned.shape[:3]
    half, wide = size // 2, size * 2
    panel = left_cols.shape[0]
    cell = panel // cols_axis
    inner, terms = right_cols.shape
    kept = kept_cols.shape[1]
    body = parts * half
    sds = jax.ShapeDtypeStruct

    chips = rows_axis // 2

    def turn(count, by):
        return [(i, (i + by) % count) for i in range(count)]

    def along(by):
        return [(i, (i + 2 * by) % rows_axis) for i in range(rows_axis)]

    swap = [(i, i ^ 1) for i in range(rows_axis)]
    def hops(by):
        return [(i, (i + (-2 if i % 2 else 2) * by) % rows_axis) for i in range(rows_axis)]

    def ring(x):
        return lax.ppermute(x, "row", hops(1))

    def swapped(x):
        return lax.ppermute(x, "row", swap)

    right = pl.pallas_call(
        pack_right_kernel,
        out_shape=sds((right_blocks.shape[0] * terms, half, wide), F32),
        in_specs=[vspec()],
        out_specs=vspec(),
        compiler_params=limit(4),
        name="pack_right",
    )(right_blocks)
    right_two = swapped(right)

    opposite = chips // 2
    self_rows, keep, give = pl.pallas_call(
        functools.partial(pack_left_kernel, panel),
        out_shape=(sds((2, body + 8, wide), F32),) + (sds((chips - 1, body + 8, wide), F32),) * 2,
        in_specs=[sspec(), vspec()],
        out_specs=(vspec(),) * 3,
        scratch_shapes=[SMEM((rows_axis,), jnp.int32)],
        compiler_params=limit(8),
        name="pack_left",
    )(owned_rows, ks_owned)
    sent = pl.pallas_call(
        join_left_kernel,
        out_shape=tuple(
            sds((2 if hop == opposite else 4, body + 8, wide), F32) for hop in range(1, opposite + 1)
        ),
        in_specs=[vspec()] * 2 + [aspec()],
        out_specs=(vspec(),) * opposite,
        compiler_params=limit(6),
        name="join_left",
    )(keep, swapped(give), right_two)
    arrived = [self_rows] + [None] * opposite
    for hop in range(opposite, 0, -1):
        arrived[hop] = lax.ppermute(sent[hop - 1], "row", hops(hop))

    list_size = panel * parts * terms + 8
    pair_list = pl.pallas_call(
        functools.partial(pairs_kernel, chips),
        out_shape=sds((list_size,), jnp.int32),
        in_specs=[sspec()] * 3,
        out_specs=sspec(),
        scratch_shapes=[SMEM((inner,), jnp.int32)],
        compiler_params=limit(1),
        name="pairs",
    )(left_cols.T, right_cols.T, kept_cols.T)

    own_rows, other_rows = pl.pallas_call(
        functools.partial(compact_kernel, panel),
        out_shape=(sds((cell, body, wide), F32),) * 2,
        in_specs=[vspec()] * len(arrived) + [aspec()],
        out_specs=(vspec(), vspec()),
        compiler_params=limit(6),
        name="compact",
    )(*arrived, pair_list)
    mine = own_rows + lax.ppermute(other_rows, "row", swap)

    rows_of = cell * parts
    mine = mine.reshape(rows_of, half, wide)
    above = lax.ppermute(mine, "col", turn(cols_axis, -1))
    below = lax.ppermute(mine, "col", turn(cols_axis, 1))
    first_half = lax.ppermute(below[: rows_of // 2], "col", turn(cols_axis, 1))
    second_half = lax.ppermute(above[rows_of // 2 :], "col", turn(cols_axis, -1))
    first_half = gate(first_half, second_half, flops=10000000000)
    lefts = [(mine, 0, 0), (above, 1, 0), (below, 3, 0), (first_half, 2, 0), (second_half, 2, rows_of // 2)]

    def joined(a, b):
        return pl.pallas_call(
            join_kernel,
            out_shape=sds((2 * a.shape[0],) + a.shape[1:], F32),
            in_specs=[vspec()] * 2,
            out_specs=vspec(),
            compiler_params=limit(4),
            name="join",
        )(a, b)

    a1, b1 = ring(right), gate(ring(right_two), mine)
    a2, b2 = ring(a1), ring(b1)
    a3, b3 = ring(a2), ring(b2)
    a4 = ring(a3)
    rights = [right, right_two, a1, a2, a3, a4, b1, b2, b3]
    rights += [swapped(joined(a1, b1)), swapped(joined(a2, b2)), swapped(joined(a3, b3)), swapped(a4)]

    blocks = cell * kept

    def products(spec):
        def kernel(list_ref, *refs):
            n_out = sum(len(ranges) for _, ranges in spec)
            outs = list(refs[len(lefts) + len(rights) :][:n_out])
            chunks = []
            for t, ranges in spec:
                chunks.append((t, [(outs.pop(0), lohi) for lohi in ranges]))
            product_kernel(chunks, [place for _, *place in lefts], len(rights), list_ref, *refs)

        shapes = tuple(sds((hi - lo, half, wide), F32) for _, ranges in spec for lo, hi in ranges)
        return pl.pallas_call(
            kernel,
            out_shape=shapes,
            in_specs=[sspec()] + [vspec()] * (len(lefts) + len(rights)),
            out_specs=tuple(vspec() for _ in shapes),
            scratch_shapes=[
                VMEM((panel * parts, half, wide), F32),
                VMEM((GROUP, half, wide), F32),
            ],
            compiler_params=limit(20),
            name="products",
        )(pair_list, *[x for x, _, _ in lefts], *rights)

    mid = blocks // 2
    lower, upper = (0, mid), (mid, blocks)
    up, down = turn(layers, 1), turn(layers, -1)
    far_a, far_b = products([(0, [lower, upper])])
    got_a = lax.ppermute(far_a, "layer", up)
    got_b = lax.ppermute(far_b, "layer", down)
    one_a, one_b, three_a, three_b = products([(1, [lower, upper]), (2, [lower, upper])])
    (own,) = products([(3, [(0, blocks)])])
    from_low_b = lax.ppermute(one_b, "layer", up)
    from_high_a = lax.ppermute(three_a, "layer", down)
    from_low_a = lax.ppermute(one_a + got_a, "layer", up)
    from_high_b = lax.ppermute(three_b + got_b, "layer", down)
    return pl.pallas_call(
        final_kernel,
        out_shape=sds((cell, kept, size, size), F32),
        in_specs=[vspec()] * 5,
        out_specs=vspec(),
        compiler_params=limit(8),
        name="final",
    )(own, from_low_a, from_low_b, from_high_a, from_high_b)


def solution(mesh):
    placed = (
        P(("row", "col"), "layer", None, None),
        P(("row", "col")),
        P("row", "layer"),
        P(("layer", "row"), "col", None, None),
        P("layer", "col"),
        P("row", "col"),
    )
    return jax.shard_map(
        shards,
        mesh=mesh,
        in_specs=placed,
        out_specs=P(("row", "layer"), "col", None, None),
        check_vma=False,
    )
```

```python
import functools

import jax
import jax.numpy as jnp
from jax import lax
from jax.experimental import pallas as pl
from jax.experimental.pallas import tpu as pltpu
from jax.sharding import PartitionSpec as P

VMEM = pltpu.VMEM
SMEM = pltpu.SMEM
GROUP = 8
CHUNKS = (2, 1, 3, 0)
F32 = jnp.float32
BF16 = jnp.bfloat16


def vspec():
    return pl.BlockSpec(memory_space=VMEM)


def sspec():
    return pl.BlockSpec(memory_space=SMEM)


def aspec():
    return pl.BlockSpec(memory_space=pl.ANY)


def limit(mib):
    return pltpu.CompilerParams(vmem_limit_bytes=mib << 20)


def folded(block):
    half = block.shape[0] // 2
    return jnp.concatenate([block[:half], block[half:]], axis=1)


def pack_right_kernel(blocks_ref, out_ref):
    rows, slots = blocks_ref.shape[:2]
    for i in range(rows):
        for k in range(slots):
            out_ref[i * slots + k] = folded(blocks_ref[i, k])


def pack_left_kernel(span, owned_ref, blocks_ref, self_ref, keep_ref, give_ref, slot_of):
    slots, parts, size = blocks_ref.shape[:3]
    groups = slot_of.shape[0]
    chips = groups // 2
    half = size // 2
    body = parts * half
    row = lax.axis_index("row")
    chip, core = lax.div(row, 2), lax.rem(row, 2)

    for g in range(groups):
        slot_of[g] = -1

    def find(s, carry):
        row = owned_ref[s]

        @pl.when(row >= 0)
        def _():
            slot_of[lax.div(row, span)] = s

        return carry

    lax.fori_loop(0, slots, find, 0)

    def put(out_ref, n, to_chip, to_core):
        slot = slot_of[to_chip * 2 + to_core]
        at = jnp.maximum(slot, 0)
        number = jnp.where(slot >= 0, owned_ref[at], -1).astype(F32)
        numbers = out_ref.shape[0] - 8
        out_ref[numbers + n : numbers + n + 1, :] = jnp.full((1, 2 * size), number, F32)
        for k in range(parts):
            out_ref[n * body + k * half : n * body + (k + 1) * half, :] = folded(blocks_ref[at, k])

    for out_ref, carrier in ((give_ref, 1 - core), (keep_ref, core)):
        for hop in range(1, chips // 2):
            to_chip = lax.rem(chip + chips + hop - 2 * hop * carrier, chips)
            put(out_ref, 2 * hop - 2, to_chip, 0)
            put(out_ref, 2 * hop - 1, to_chip, 1)
        put(out_ref, chips - 2, lax.rem(chip + chips // 2, chips), carrier)
    put(self_ref, 0, chip, 0)
    put(self_ref, 1, chip, 1)


def join_left_kernel(body, keep_ref, got_ref, after_ref, *out_refs):
    at = 0
    for ref in out_refs:
        count = (ref.shape[0] - 8) // (2 * body)
        numbers = ref.shape[0] - 8
        ref[numbers:, :] = jnp.full((8, ref.shape[1]), -1.0, F32)
        for n, source in enumerate((keep_ref, got_ref)):
            ref[n * count * body : (n + 1) * count * body, :] = source[at * body : (at + count) * body, :]
            first = source.shape[0] - 8 + at
            ref[numbers + n * count : numbers + (n + 1) * count, :] = source[first : first + count, :]
        at += count


def join_kernel(first_ref, second_ref, out_ref):
    count = first_ref.shape[0]
    out_ref[:count] = first_ref[...]
    out_ref[count:] = second_ref[...]


def compact_kernel(span, *refs):
    arrived, (own_ref, other_ref) = refs[:-3], refs[-2:]
    cell, body = own_ref.shape[:2]
    row = lax.axis_index("row")
    core = lax.rem(row, 2)
    own = [(arrived[0], core)] + [(ref, n + core) for ref in arrived[1:-1] for n in (0, 2)]
    own += [(arrived[-1], n) for n in range(2)]
    other = [(arrived[0], 1 - core)] + [(ref, n + 1 - core) for ref in arrived[1:-1] for n in (0, 2)]
    sides = ((own_ref, own, row), (other_ref, other, row + 1 - 2 * core))

    def number_of(ref, n):
        tile = ref[ref.shape[0] - 8 :, :]
        at = lax.broadcasted_iota(jnp.int32, tile.shape, 0)
        return jnp.max(jnp.where(at == n, tile, -1.0)).astype(jnp.int32)

    numbers = [[number_of(ref, n) for ref, n in side] for _, side, _ in sides]
    own_ref[...] = jnp.zeros_like(own_ref)
    other_ref[...] = jnp.zeros_like(other_ref)
    for (out_ref, side, to), found in zip(sides, numbers):
        first = to * span + lax.axis_index("col") * cell
        for (ref, n), number in zip(side, found):

            @pl.when(number >= 0)
            def _(out_ref=out_ref, first=first, ref=ref, n=n, number=number):
                out_ref[number - first] = ref[pl.ds(pl.multiple_of(n * body, body), body), :]


def gate(array, *after, flops=0):
    return pl.pallas_call(
        lambda *refs: None,
        out_shape=jax.ShapeDtypeStruct(array.shape, array.dtype),
        in_specs=[aspec()] * (1 + len(after)),
        out_specs=aspec(),
        input_output_aliases={0: 0},
        compiler_params=limit(1),
        cost_estimate=pl.CostEstimate(flops=flops, bytes_accessed=0, transcendentals=0),
        name="gate",
    )(array, *after)


def pairs_kernel(chips, left_ref, right_ref, kept_ref, list_ref, table):
    parts, rows = left_ref.shape
    terms, inner = right_ref.shape
    kept = kept_ref.shape[0]
    layers = len(CHUNKS)
    cell = rows // layers
    layer = lax.axis_index("layer")
    left_first = layer * inner
    per_device = inner // (2 * chips)
    chip = lax.div(lax.axis_index("row"), 2)
    core = lax.rem(lax.axis_index("row"), 2)
    right_first = lax.axis_index("col") * table.shape[0]

    def clear(i, carry):
        table[i] = -1
        return carry

    lax.fori_loop(0, table.shape[0], clear, 0)
    count = 0
    for t, distance in enumerate(CHUNKS):
        list_ref[list_ref.shape[0] - 8 + t] = count
        base = lax.rem(layer + distance, layers) * cell

        def one_row(p, count, base=base):
            r = base + p
            for q in range(kept):
                table[kept_ref[q, r] - right_first] = q
            for k in range(parts):
                j = left_ref[k, r] - left_first
                source = lax.div(j, per_device)
                of_core = lax.rem(source, 2)
                away = lax.rem(lax.div(source, 2) - chip + chips, chips)
                ahead = jnp.where(away * 2 == chips, of_core, (away * 2 < chips).astype(jnp.int32))
                hops = jnp.where(away * 2 <= chips, away, chips - away)
                far = chips // 2
                held = 1 + hops
                second = (ahead != of_core).astype(jnp.int32)
                crossed = (ahead != core).astype(jnp.int32)
                held = held + jnp.where(crossed == 1, 2 * far - 1, far * second)
                held = jnp.where(hops == 0, jnp.where(of_core == core, 0, 1), held)
                first_block = (crossed * second * per_device + lax.rem(j, per_device)) * terms
                first_block = jnp.where(hops == 0, lax.rem(j, per_device) * terms, first_block)
                base_code = (p * parts + k) + held * 128 + first_block * 2048
                for l in range(terms):
                    q = table[right_ref[l, j] - right_first]
                    code = base_code + l * 2048 + (p * kept + q) * 131072
                    list_ref[count] = code
                    count = count + (q >= 0).astype(jnp.int32)
            for q in range(kept):
                table[kept_ref[q, r] - right_first] = -1
            return count

        count = lax.fori_loop(0, cell, one_row, count)
    list_ref[list_ref.shape[0] - 8 + layers] = count


def product_kernel(chunks, places, n_right, list_ref, *refs):
    left_refs, right_refs = refs[: len(places)], refs[len(places) : len(places) + n_right]
    left, ring = refs[-2:]
    layers = len(CHUNKS)
    col, layer = lax.axis_index("col"), lax.axis_index("layer")

    def start_of(t):
        return list_ref[list_ref.shape[0] - 8 + t]

    def field(code, shift, bits):
        return lax.shift_right_logical(code, shift) & ((1 << bits) - 1)

    for _, targets in chunks:
        for ref, _ in targets:
            ref[...] = jnp.zeros_like(ref)

    def fetch(code, u):
        held, block = field(code, 7, 4), field(code, 11, 6)

        def choose(lo, hi):
            if hi - lo == 1:
                ring[u] = right_refs[lo][block]
                return
            mid = (lo + hi) // 2

            @pl.when(held < mid)
            def _():
                choose(lo, mid)

            @pl.when(held >= mid)
            def _():
                choose(mid, hi)

        choose(0, n_right)

    half, wide = ring.shape[1:]
    low = lax.broadcasted_iota(jnp.int32, (half, wide), 1) < half * 2

    def product(code, u):
        a = left[field(code, 0, 5)]
        b = ring[u]
        turned = pltpu.roll(b, wide // 2, 1)
        full = jnp.concatenate(
            [
                jnp.where(low, b, 0.0),
                jnp.where(low, turned, 0.0),
                jnp.where(low, 0.0, turned),
                jnp.where(low, 0.0, b),
            ],
            axis=0,
        )
        a_hi = a.astype(BF16)
        a_lo = (a - a_hi.astype(F32)).astype(BF16)
        f_hi = full.astype(BF16)
        f_lo = (full - f_hi.astype(F32)).astype(BF16)
        main = jnp.dot(a_hi, f_hi, preferred_element_type=F32)
        rest = jnp.dot(a_lo, f_hi, preferred_element_type=F32) + jnp.dot(
            a_hi, f_lo, preferred_element_type=F32
        )
        return main + rest

    for t, targets in chunks:
        start, stop = start_of(t), start_of(t + 1)
        source = lax.rem(layer + CHUNKS[t] - col + layers, layers)
        for n, (further, first_row) in enumerate(places):

            @pl.when(source == further)
            def _(n=n, first_row=first_row):
                left[first_row : first_row + left_refs[n].shape[0]] = left_refs[n][...]


        def group(g, carry, start=start, stop=stop, targets=targets):
            base = start + g * GROUP
            codes = [list_ref[jnp.minimum(base + u, stop - 1)] for u in range(GROUP)]
            for u in range(GROUP):
                fetch(codes[u], u)
            values = [product(codes[u], u) for u in range(GROUP)]
            for u in range(GROUP):
                spot = field(codes[u], 17, 6)
                for ref, (lo, hi) in targets:

                    @pl.when((base + u < stop) & (spot >= lo) & (spot < hi))
                    def _(u=u, ref=ref, lo=lo, spot=spot):
                        ref[spot - lo] += values[u]

            return carry

        lax.fori_loop(0, lax.div(stop - start + GROUP - 1, GROUP), group, 0)


def final_kernel(own_ref, a0, a1, b0, b1, out_ref):
    rows, kept, size = out_ref.shape[:3]
    half = size // 2
    per = a0.shape[0]

    for i in range(rows * kept):
        p, q = i // kept, i % kept
        x, y = (a0, b0) if i < per else (a1, b1)
        total = own_ref[i] + x[i % per] + y[i % per]
        out_ref[p, q, :half, :] = total[:, :size]
        out_ref[p, q, half:, :] = total[:, size:]


def shards(ks_owned, owned_rows, left_cols, right_blocks, right_cols, kept_cols):
    rows_axis = lax.axis_size("row")
    cols_axis = lax.axis_size("col")
    layers = lax.axis_size("layer")
    slots, parts, size = ks_owned.shape[:3]
    half, wide = size // 2, size * 2
    panel = left_cols.shape[0]
    cell = panel // cols_axis
    inner, terms = right_cols.shape
    kept = kept_cols.shape[1]
    body = parts * half
    sds = jax.ShapeDtypeStruct

    chips = rows_axis // 2

    def turn(count, by):
        return [(i, (i + by) % count) for i in range(count)]

    def along(by):
        return [(i, (i + 2 * by) % rows_axis) for i in range(rows_axis)]

    swap = [(i, i ^ 1) for i in range(rows_axis)]
    def hops(by):
        return [(i, (i + (-2 if i % 2 else 2) * by) % rows_axis) for i in range(rows_axis)]

    def ring(x):
        return lax.ppermute(x, "row", hops(1))

    def swapped(x):
        return lax.ppermute(x, "row", swap)

    right = pl.pallas_call(
        pack_right_kernel,
        out_shape=sds((right_blocks.shape[0] * terms, half, wide), F32),
        in_specs=[vspec()],
        out_specs=vspec(),
        compiler_params=limit(4),
        name="pack_right",
    )(right_blocks)
    right_two = swapped(right)

    opposite = chips // 2
    self_rows, keep, give = pl.pallas_call(
        functools.partial(pack_left_kernel, panel),
        out_shape=(sds((2 * body + 8, wide), F32),) + (sds(((chips - 1) * body + 8, wide), F32),) * 2,
        in_specs=[sspec(), vspec()],
        out_specs=(vspec(),) * 3,
        scratch_shapes=[SMEM((rows_axis,), jnp.int32)],
        compiler_params=limit(8),
        name="pack_left",
    )(jnp.maximum(owned_rows, -1), ks_owned)
    sent = pl.pallas_call(
        functools.partial(join_left_kernel, body),
        out_shape=tuple(
            sds(((2 if hop == opposite else 4) * body + 8, wide), F32) for hop in range(1, opposite + 1)
        ),
        in_specs=[vspec()] * 2 + [aspec()],
        out_specs=(vspec(),) * opposite,
        compiler_params=limit(6),
        name="join_left",
    )(keep, swapped(give), right_two)
    arrived = [self_rows] + [None] * opposite
    for hop in range(opposite, 0, -1):
        arrived[hop] = lax.ppermute(sent[hop - 1], "row", hops(hop))

    list_size = panel * parts * terms + 8
    pair_list = pl.pallas_call(
        functools.partial(pairs_kernel, chips),
        out_shape=sds((list_size,), jnp.int32),
        in_specs=[sspec()] * 3,
        out_specs=sspec(),
        scratch_shapes=[SMEM((inner,), jnp.int32)],
        compiler_params=limit(1),
        name="pairs",
    )(left_cols.T, right_cols.T, kept_cols.T)

    own_rows, other_rows = pl.pallas_call(
        functools.partial(compact_kernel, panel),
        out_shape=(sds((cell, body, wide), F32),) * 2,
        in_specs=[vspec()] * len(arrived) + [aspec()],
        out_specs=(vspec(), vspec()),
        compiler_params=limit(6),
        name="compact",
    )(*arrived, pair_list)
    mine = own_rows + lax.ppermute(other_rows, "row", swap)

    rows_of = cell * parts
    mine = mine.reshape(rows_of, half, wide)
    above = lax.ppermute(mine, "col", turn(cols_axis, -1))
    below = lax.ppermute(mine, "col", turn(cols_axis, 1))
    first_half = lax.ppermute(below[: rows_of // 2], "col", turn(cols_axis, 1))
    second_half = lax.ppermute(above[rows_of // 2 :], "col", turn(cols_axis, -1))
    first_half = gate(first_half, second_half, flops=10000000000)
    lefts = [(mine, 0, 0), (above, 1, 0), (below, 3, 0), (first_half, 2, 0), (second_half, 2, rows_of // 2)]

    def joined(a, b):
        return pl.pallas_call(
            join_kernel,
            out_shape=sds((2 * a.shape[0],) + a.shape[1:], F32),
            in_specs=[vspec()] * 2,
            out_specs=vspec(),
            compiler_params=limit(4),
            name="join",
        )(a, b)

    a1, b1 = ring(right), gate(ring(right_two), mine)
    a2, b2 = ring(a1), ring(b1)
    a3, b3 = ring(a2), ring(b2)
    a4 = ring(a3)
    rights = [right, right_two, a1, a2, a3, a4, b1, b2, b3]
    rights += [swapped(joined(a1, b1)), swapped(joined(a2, b2)), swapped(joined(a3, b3)), swapped(a4)]

    blocks = cell * kept

    def products(spec):
        def kernel(list_ref, *refs):
            n_out = sum(len(ranges) for _, ranges in spec)
            outs = list(refs[len(lefts) + len(rights) :][:n_out])
            chunks = []
            for t, ranges in spec:
                chunks.append((t, [(outs.pop(0), lohi) for lohi in ranges]))
            product_kernel(chunks, [place for _, *place in lefts], len(rights), list_ref, *refs)

        shapes = tuple(sds((hi - lo, half, wide), F32) for _, ranges in spec for lo, hi in ranges)
        return pl.pallas_call(
            kernel,
            out_shape=shapes,
            in_specs=[sspec()] + [vspec()] * (len(lefts) + len(rights)),
            out_specs=tuple(vspec() for _ in shapes),
            scratch_shapes=[
                VMEM((cell * parts, half, wide), F32),
                VMEM((GROUP, half, wide), F32),
            ],
            compiler_params=limit(20),
            name="products",
        )(pair_list, *[x for x, _, _ in lefts], *rights)

    mid = blocks // 2
    lower, upper = (0, mid), (mid, blocks)
    up, down = turn(layers, 1), turn(layers, -1)
    far_a, far_b = products([(0, [lower, upper])])
    got_a = lax.ppermute(far_a, "layer", up)
    got_b = lax.ppermute(far_b, "layer", down)
    one_a, one_b, three_a, three_b = products([(1, [lower, upper]), (2, [lower, upper])])
    (own,) = products([(3, [(0, blocks)])])
    from_low_b = lax.ppermute(one_b, "layer", up)
    from_high_a = lax.ppermute(three_a, "layer", down)
    from_low_a = lax.ppermute(one_a + got_a, "layer", up)
    from_high_b = lax.ppermute(three_b + got_b, "layer", down)
    return pl.pallas_call(
        final_kernel,
        out_shape=sds((cell, kept, size, size), F32),
        in_specs=[vspec()] * 5,
        out_specs=vspec(),
        compiler_params=limit(8),
        name="final",
    )(own, from_low_a, from_low_b, from_high_a, from_high_b)


def solution(mesh):
    placed = (
        P(("row", "col"), "layer", None, None),
        P(("row", "col")),
        P("row", "layer"),
        P(("layer", "row"), "col", None, None),
        P("layer", "col"),
        P("row", "col"),
    )
    return jax.shard_map(
        shards,
        mesh=mesh,
        in_specs=placed,
        out_specs=P(("row", "layer"), "col", None, None),
        check_vma=False,
    )
```

```python
import functools

import jax
import jax.numpy as jnp
from jax import lax
from jax.experimental import pallas as pl
from jax.experimental.pallas import tpu as pltpu
from jax.sharding import PartitionSpec as P

VMEM = pltpu.VMEM
SMEM = pltpu.SMEM
GROUP = 8
CHUNKS = (2, 1, 3, 0)
F32 = jnp.float32
BF16 = jnp.bfloat16


def vspec():
    return pl.BlockSpec(memory_space=VMEM)


def sspec():
    return pl.BlockSpec(memory_space=SMEM)


def aspec():
    return pl.BlockSpec(memory_space=pl.ANY)


def limit(mib):
    return pltpu.CompilerParams(vmem_limit_bytes=mib << 20)


def folded(block):
    half = block.shape[0] // 2
    return jnp.concatenate([block[:half], block[half:]], axis=1)


def pack_right_kernel(blocks_ref, out_ref):
    rows, slots = blocks_ref.shape[:2]
    for i in range(rows):
        for k in range(slots):
            out_ref[i * slots + k] = folded(blocks_ref[i, k])


def pack_left_kernel(span, owned_ref, blocks_ref, self_ref, keep_ref, give_ref, slot_of):
    slots, parts, size = blocks_ref.shape[:3]
    groups = slot_of.shape[0]
    chips = groups // 2
    half = size // 2
    body = parts * half
    row = lax.axis_index("row")
    chip, core = lax.div(row, 2), lax.rem(row, 2)

    for g in range(groups):
        slot_of[g] = -1

    def find(s, carry):
        row = owned_ref[s]

        @pl.when(row >= 0)
        def _():
            slot_of[lax.div(row, span)] = s

        return carry

    lax.fori_loop(0, slots, find, 0)

    def put(out_ref, n, to_chip, to_core):
        slot = slot_of[to_chip * 2 + to_core]
        at = jnp.maximum(slot, 0)
        number = jnp.where(slot >= 0, owned_ref[at], -1).astype(F32)
        numbers = out_ref.shape[0] - 8
        out_ref[numbers + n : numbers + n + 1, :] = jnp.full((1, 2 * size), number, F32)
        for k in range(parts):
            out_ref[n * body + k * half : n * body + (k + 1) * half, :] = folded(blocks_ref[at, k])

    for out_ref, carrier in ((give_ref, 1 - core), (keep_ref, core)):
        for hop in range(1, chips // 2):
            to_chip = lax.rem(chip + chips + hop - 2 * hop * carrier, chips)
            put(out_ref, 2 * hop - 2, to_chip, 0)
            put(out_ref, 2 * hop - 1, to_chip, 1)
        put(out_ref, chips - 2, lax.rem(chip + chips // 2, chips), carrier)
    put(self_ref, 0, chip, 0)
    put(self_ref, 1, chip, 1)


def join_left_kernel(body, keep_ref, got_ref, after_ref, *out_refs):
    at = 0
    for ref in out_refs:
        count = (ref.shape[0] - 8) // (2 * body)
        numbers = ref.shape[0] - 8
        ref[numbers:, :] = jnp.full((8, ref.shape[1]), -1.0, F32)
        for n, source in enumerate((keep_ref, got_ref)):
            ref[n * count * body : (n + 1) * count * body, :] = source[at * body : (at + count) * body, :]
            first = source.shape[0] - 8 + at
            ref[numbers + n * count : numbers + (n + 1) * count, :] = source[first : first + count, :]
        at += count


def join_kernel(first_ref, second_ref, out_ref):
    count = first_ref.shape[0]
    out_ref[:count] = first_ref[...]
    out_ref[count:] = second_ref[...]


def compact_kernel(span, *refs):
    arrived, (own_ref, other_ref) = refs[:-3], refs[-2:]
    cell, body = own_ref.shape[:2]
    row = lax.axis_index("row")
    core = lax.rem(row, 2)
    own = [(arrived[0], core)] + [(ref, n + core) for ref in arrived[1:-1] for n in (0, 2)]
    own += [(arrived[-1], n) for n in range(2)]
    other = [(arrived[0], 1 - core)] + [(ref, n + 1 - core) for ref in arrived[1:-1] for n in (0, 2)]
    sides = ((own_ref, own, row), (other_ref, other, row + 1 - 2 * core))

    def number_of(ref, n):
        tile = ref[ref.shape[0] - 8 :, :]
        at = lax.broadcasted_iota(jnp.int32, tile.shape, 0)
        return jnp.max(jnp.where(at == n, tile, -1.0)).astype(jnp.int32)

    numbers = [[number_of(ref, n) for ref, n in side] for _, side, _ in sides]
    own_ref[...] = jnp.zeros_like(own_ref)
    other_ref[...] = jnp.zeros_like(other_ref)
    for (out_ref, side, to), found in zip(sides, numbers):
        first = to * span + lax.axis_index("col") * cell
        for (ref, n), number in zip(side, found):

            @pl.when(number >= 0)
            def _(out_ref=out_ref, first=first, ref=ref, n=n, number=number):
                out_ref[number - first] = ref[pl.ds(pl.multiple_of(n * body, body), body), :]


def gate(array, *after, flops=0):
    return pl.pallas_call(
        lambda *refs: None,
        out_shape=jax.ShapeDtypeStruct(array.shape, array.dtype),
        in_specs=[aspec()] * (1 + len(after)),
        out_specs=aspec(),
        input_output_aliases={0: 0},
        compiler_params=limit(1),
        cost_estimate=pl.CostEstimate(flops=flops, bytes_accessed=0, transcendentals=0),
        name="gate",
    )(array, *after)


def pairs_kernel(chips, left_ref, right_ref, kept_ref, list_ref, table):
    parts, rows = left_ref.shape
    terms, inner = right_ref.shape
    kept = kept_ref.shape[0]
    layers = len(CHUNKS)
    cell = rows // layers
    layer = lax.axis_index("layer")
    left_first = layer * inner
    per_device = inner // (2 * chips)
    chip = lax.div(lax.axis_index("row"), 2)
    core = lax.rem(lax.axis_index("row"), 2)
    right_first = lax.axis_index("col") * table.shape[0]

    def clear(i, carry):
        table[i] = -1
        return carry

    lax.fori_loop(0, table.shape[0], clear, 0)
    count = 0
    for t, distance in enumerate(CHUNKS):
        list_ref[list_ref.shape[0] - 8 + t] = count
        base = lax.rem(layer + distance, layers) * cell

        def one_row(p, count, base=base):
            r = base + p
            for q in range(kept):
                table[kept_ref[q, r] - right_first] = q
            for k in range(parts):
                j = left_ref[k, r] - left_first
                source = lax.div(j, per_device)
                of_core = lax.rem(source, 2)
                away = lax.rem(lax.div(source, 2) - chip + chips, chips)
                ahead = jnp.where(away * 2 == chips, of_core, (away * 2 < chips).astype(jnp.int32))
                hops = jnp.where(away * 2 <= chips, away, chips - away)
                far = chips // 2
                held = 1 + hops
                second = (ahead != of_core).astype(jnp.int32)
                crossed = (ahead != core).astype(jnp.int32)
                held = held + jnp.where(crossed == 1, 2 * far - 1, far * second)
                held = jnp.where(hops == 0, jnp.where(of_core == core, 0, 1), held)
                first_block = (crossed * second * per_device + lax.rem(j, per_device)) * terms
                first_block = jnp.where(hops == 0, lax.rem(j, per_device) * terms, first_block)
                base_code = (p * parts + k) + held * 128 + first_block * 2048
                for l in range(terms):
                    q = table[right_ref[l, j] - right_first]
                    code = base_code + l * 2048 + (p * kept + q) * 131072
                    list_ref[count] = code
                    count = count + (q >= 0).astype(jnp.int32)
            for q in range(kept):
                table[kept_ref[q, r] - right_first] = -1
            return count

        count = lax.fori_loop(0, cell, one_row, count)
    list_ref[list_ref.shape[0] - 8 + layers] = count


def product_kernel(chunks, places, n_right, list_ref, *refs):
    left_refs, right_refs = refs[: len(places)], refs[len(places) : len(places) + n_right]
    left, ring = refs[-2:]
    layers = len(CHUNKS)
    col, layer = lax.axis_index("col"), lax.axis_index("layer")

    def start_of(t):
        return list_ref[list_ref.shape[0] - 8 + t]

    def field(code, shift, bits):
        return lax.shift_right_logical(code, shift) & ((1 << bits) - 1)

    for _, targets in chunks:
        for ref, _ in targets:
            ref[...] = jnp.zeros_like(ref)

    def fetch(code, u):
        held, block = field(code, 7, 4), field(code, 11, 6)

        def choose(lo, hi):
            if hi - lo == 1:
                ring[u] = right_refs[lo][block]
                return
            mid = (lo + hi) // 2

            @pl.when(held < mid)
            def _():
                choose(lo, mid)

            @pl.when(held >= mid)
            def _():
                choose(mid, hi)

        choose(0, n_right)

    half, wide = ring.shape[1:]
    low = lax.broadcasted_iota(jnp.int32, (half, wide), 1) < half * 2

    def product(code, u):
        a = left[field(code, 0, 5)]
        b = ring[u]
        turned = pltpu.roll(b, wide // 2, 1)
        full = jnp.concatenate(
            [
                jnp.where(low, b, 0.0),
                jnp.where(low, turned, 0.0),
                jnp.where(low, 0.0, turned),
                jnp.where(low, 0.0, b),
            ],
            axis=0,
        )
        a_hi = a.astype(BF16)
        a_lo = (a - a_hi.astype(F32)).astype(BF16)
        f_hi = full.astype(BF16)
        f_lo = (full - f_hi.astype(F32)).astype(BF16)
        both = jnp.dot(jnp.concatenate([a_hi, a_lo], axis=0), f_hi, preferred_element_type=F32)
        return both[:half] + (both[half:] + jnp.dot(a_hi, f_lo, preferred_element_type=F32))

    for t, targets in chunks:
        start, stop = start_of(t), start_of(t + 1)
        source = lax.rem(layer + CHUNKS[t] - col + layers, layers)
        for n, (further, first_row) in enumerate(places):

            @pl.when(source == further)
            def _(n=n, first_row=first_row):
                left[first_row : first_row + left_refs[n].shape[0]] = left_refs[n][...]


        def group(g, carry, start=start, stop=stop, targets=targets):
            base = start + g * GROUP
            codes = [list_ref[jnp.minimum(base + u, stop - 1)] for u in range(GROUP)]
            for u in range(GROUP):
                fetch(codes[u], u)
            values = [product(codes[u], u) for u in range(GROUP)]
            for u in range(GROUP):
                spot = field(codes[u], 17, 6)
                for ref, (lo, hi) in targets:

                    @pl.when((base + u < stop) & (spot >= lo) & (spot < hi))
                    def _(u=u, ref=ref, lo=lo, spot=spot):
                        ref[spot - lo] += values[u]

            return carry

        lax.fori_loop(0, lax.div(stop - start + GROUP - 1, GROUP), group, 0)


def final_kernel(own_ref, a0, a1, b0, b1, out_ref):
    rows, kept, size = out_ref.shape[:3]
    half = size // 2
    per = a0.shape[0]

    for i in range(rows * kept):
        p, q = i // kept, i % kept
        x, y = (a0, b0) if i < per else (a1, b1)
        total = own_ref[i] + x[i % per] + y[i % per]
        out_ref[p, q, :half, :] = total[:, :size]
        out_ref[p, q, half:, :] = total[:, size:]


def shards(ks_owned, owned_rows, left_cols, right_blocks, right_cols, kept_cols):
    rows_axis = lax.axis_size("row")
    cols_axis = lax.axis_size("col")
    layers = lax.axis_size("layer")
    slots, parts, size = ks_owned.shape[:3]
    half, wide = size // 2, size * 2
    panel = left_cols.shape[0]
    cell = panel // cols_axis
    inner, terms = right_cols.shape
    kept = kept_cols.shape[1]
    body = parts * half
    sds = jax.ShapeDtypeStruct

    chips = rows_axis // 2

    def turn(count, by):
        return [(i, (i + by) % count) for i in range(count)]

    def along(by):
        return [(i, (i + 2 * by) % rows_axis) for i in range(rows_axis)]

    swap = [(i, i ^ 1) for i in range(rows_axis)]
    def hops(by):
        return [(i, (i + (-2 if i % 2 else 2) * by) % rows_axis) for i in range(rows_axis)]

    def ring(x):
        return lax.ppermute(x, "row", hops(1))

    def swapped(x):
        return lax.ppermute(x, "row", swap)

    right = pl.pallas_call(
        pack_right_kernel,
        out_shape=sds((right_blocks.shape[0] * terms, half, wide), F32),
        in_specs=[vspec()],
        out_specs=vspec(),
        compiler_params=limit(4),
        name="pack_right",
    )(right_blocks)
    right_two = swapped(right)

    opposite = chips // 2
    self_rows, keep, give = pl.pallas_call(
        functools.partial(pack_left_kernel, panel),
        out_shape=(sds((2 * body + 8, wide), F32),) + (sds(((chips - 1) * body + 8, wide), F32),) * 2,
        in_specs=[sspec(), vspec()],
        out_specs=(vspec(),) * 3,
        scratch_shapes=[SMEM((rows_axis,), jnp.int32)],
        compiler_params=limit(8),
        name="pack_left",
    )(jnp.maximum(owned_rows, -1), ks_owned)
    sent = pl.pallas_call(
        functools.partial(join_left_kernel, body),
        out_shape=tuple(
            sds(((2 if hop == opposite else 4) * body + 8, wide), F32) for hop in range(1, opposite + 1)
        ),
        in_specs=[vspec()] * 2 + [aspec()],
        out_specs=(vspec(),) * opposite,
        compiler_params=limit(6),
        name="join_left",
    )(keep, swapped(give), right_two)
    arrived = [self_rows] + [None] * opposite
    for hop in range(opposite, 0, -1):
        arrived[hop] = lax.ppermute(sent[hop - 1], "row", hops(hop))

    list_size = panel * parts * terms + 8
    pair_list = pl.pallas_call(
        functools.partial(pairs_kernel, chips),
        out_shape=sds((list_size,), jnp.int32),
        in_specs=[sspec()] * 3,
        out_specs=sspec(),
        scratch_shapes=[SMEM((inner,), jnp.int32)],
        compiler_params=limit(1),
        name="pairs",
    )(left_cols.T, right_cols.T, kept_cols.T)

    own_rows, other_rows = pl.pallas_call(
        functools.partial(compact_kernel, panel),
        out_shape=(sds((cell, body, wide), F32),) * 2,
        in_specs=[vspec()] * len(arrived) + [aspec()],
        out_specs=(vspec(), vspec()),
        compiler_params=limit(6),
        name="compact",
    )(*arrived, pair_list)
    mine = own_rows + lax.ppermute(other_rows, "row", swap)

    rows_of = cell * parts
    mine = mine.reshape(rows_of, half, wide)
    above = lax.ppermute(mine, "col", turn(cols_axis, -1))
    below = lax.ppermute(mine, "col", turn(cols_axis, 1))
    first_half = lax.ppermute(below[: rows_of // 2], "col", turn(cols_axis, 1))
    second_half = lax.ppermute(above[rows_of // 2 :], "col", turn(cols_axis, -1))
    first_half = gate(first_half, second_half, flops=10000000000)
    lefts = [(mine, 0, 0), (above, 1, 0), (below, 3, 0), (first_half, 2, 0), (second_half, 2, rows_of // 2)]

    def joined(a, b):
        return pl.pallas_call(
            join_kernel,
            out_shape=sds((2 * a.shape[0],) + a.shape[1:], F32),
            in_specs=[vspec()] * 2,
            out_specs=vspec(),
            compiler_params=limit(4),
            name="join",
        )(a, b)

    a1, b1 = ring(right), gate(ring(right_two), mine)
    a2, b2 = ring(a1), ring(b1)
    a3, b3 = ring(a2), ring(b2)
    a4 = ring(a3)
    rights = [right, right_two, a1, a2, a3, a4, b1, b2, b3]
    rights += [swapped(joined(a1, b1)), swapped(joined(a2, b2)), swapped(joined(a3, b3)), swapped(a4)]

    blocks = cell * kept

    def products(spec):
        def kernel(list_ref, *refs):
            n_out = sum(len(ranges) for _, ranges in spec)
            outs = list(refs[len(lefts) + len(rights) :][:n_out])
            chunks = []
            for t, ranges in spec:
                chunks.append((t, [(outs.pop(0), lohi) for lohi in ranges]))
            product_kernel(chunks, [place for _, *place in lefts], len(rights), list_ref, *refs)

        shapes = tuple(sds((hi - lo, half, wide), F32) for _, ranges in spec for lo, hi in ranges)
        return pl.pallas_call(
            kernel,
            out_shape=shapes,
            in_specs=[sspec()] + [vspec()] * (len(lefts) + len(rights)),
            out_specs=tuple(vspec() for _ in shapes),
            scratch_shapes=[
                VMEM((cell * parts, half, wide), F32),
                VMEM((GROUP, half, wide), F32),
            ],
            compiler_params=limit(20),
            name="products",
        )(pair_list, *[x for x, _, _ in lefts], *rights)

    mid = blocks // 2
    lower, upper = (0, mid), (mid, blocks)
    up, down = turn(layers, 1), turn(layers, -1)
    far_a, far_b = products([(0, [lower, upper])])
    got_a = lax.ppermute(far_a, "layer", up)
    got_b = lax.ppermute(far_b, "layer", down)
    one_a, one_b, three_a, three_b = products([(1, [lower, upper]), (2, [lower, upper])])
    (own,) = products([(3, [(0, blocks)])])
    from_low_b = lax.ppermute(one_b, "layer", up)
    from_high_a = lax.ppermute(three_a, "layer", down)
    from_low_a = lax.ppermute(one_a + got_a, "layer", up)
    from_high_b = lax.ppermute(three_b + got_b, "layer", down)
    return pl.pallas_call(
        final_kernel,
        out_shape=sds((cell, kept, size, size), F32),
        in_specs=[vspec()] * 5,
        out_specs=vspec(),
        compiler_params=limit(8),
        name="final",
    )(own, from_low_a, from_low_b, from_high_a, from_high_b)


def solution(mesh):
    placed = (
        P(("row", "col"), "layer", None, None),
        P(("row", "col")),
        P("row", "layer"),
        P(("layer", "row"), "col", None, None),
        P("layer", "col"),
        P("row", "col"),
    )
    return jax.shard_map(
        shards,
        mesh=mesh,
        in_specs=placed,
        out_specs=P(("row", "layer"), "col", None, None),
        check_vma=False,
    )
```
